1024 devices in a mesh: dp: 128 (over z_lo, y, x), seq: 8 (over z_hi, core).
Axes of the slice: x: 4, y: 8, z: 16 (z_hi: 4, z_lo: 4; z = z_hi * 4 + z_lo), core: 2. Of those that a mesh axis runs over, the one named last changes fastest.
Arguments:
- qkv_input: bfloat16 [128, 1024, 7680], P('dp', 'seq'), may hold values from -24 to 24
- conv_weight: float32 [4, 7680], replicated, may hold values from -3 to 3
- out_cotangent: bfloat16 [128, 1024, 2560], P('dp', 'seq'), may hold values from -6 to 6
Outputs:
- input_grad: bfloat16 [128, 1024, 2560], P('dp', 'seq')
- weight_grad: float32 [4, 2560], P(None, 'dp')
The draws below stay inside these ranges and needn't reach their ends.
All inputs are finite; a program needn't handle non-finite values.
Results may differ from the reference program's by a relative error of at most 0.019.
Values may be sent and summed in bfloat16 or wider, within the bound.
No kernel may reach another device: no remote copies, remote signals or barrier semaphores. Data moves between devices by JAX's collectives and lax.ppermute only.
A program may use at most 64 MiB of HBM per device.

```python
import jax
import jax.numpy as jnp
from jax import lax

HEADS = 20
HEAD = 128
CONV = 4
BLOCK = 128
CH = 2560
SEQ_LEN = 1024
SEQS = 128


def strengthened(drawn, stream_key, source, target, parts, factor):
    owner, partner = [(jnp.arange(drawn.shape[position]) // (drawn.shape[position] // parts)).reshape([-1 if axis == position else 1 for axis in range(drawn.ndim)]) for position in (source, target)]
    chosen = jax.random.permutation(stream_key, parts)[partner]
    strong = (owner == chosen) | (owner == (partner + parts // 2) % parts)
    return jnp.where(strong, factor * drawn, drawn)


def level_of(own_key, extent, pieces, least, largest):
    def one(axis_at, shards_of):
        draws = jax.random.uniform(jax.random.fold_in(jax.random.fold_in(own_key, 6), axis_at), (shards_of,), jnp.float32, least / len(pieces), largest / len(pieces))
        return jnp.repeat(jnp.exp(draws), extent[axis_at] // shards_of).reshape((-1,) + (1,) * (len(extent) - axis_at - 1))

    gain = one(*pieces[0])
    for cut in pieces[1:]:
        gain = gain * one(*cut)
    return gain


def noise(rng, shape, scale, reach, pieces=(), kind=jnp.bfloat16):
    result = scale * jax.random.normal(rng, shape, jnp.float32)
    if pieces:
        result = result * level_of(rng, shape, pieces, -0.22, 0.18)
    return jnp.clip(result, -reach, reach).astype(kind)


def noise_with(own_key, shape, width, most, split, heavy, kind=jnp.bfloat16):
    values = width * jax.random.normal(own_key, shape, jnp.float32)
    if split:
        values = values * level_of(own_key, shape, split, -0.22, 0.18)
    return jnp.clip(strengthened(values, jax.random.fold_in(own_key, 3), *heavy), -most, most).astype(kind)


def setup_inputs(seed: int = 0) -> dict:
    splits = jax.random.split(jax.random.key(seed), 4)
    return {
        "qkv_input": noise_with(splits[0], (SEQS, SEQ_LEN, 3 * CH), 1.0, 24.0, ((0, 128), (1, 8)), (0, 2, 128, 5.5)),
        "conv_weight": noise(splits[1], (CONV, 3 * CH), CONV ** -0.5, 3.0, (), jnp.float32),
        "out_cotangent": noise(splits[2], (SEQS, SEQ_LEN, CH), 1.0, 6.0, ((0, 128), (1, 8))),
    }


def rounded(value):
    return lax.optimization_barrier(value.astype(jnp.bfloat16)).astype(jnp.float32)


def one_sequence(sequence, conv_weight, out_cotangent):
    length = sequence.shape[0]
    padded = jnp.pad(sequence.astype(jnp.float32), ((CONV - 1, 0), (0, 0)))
    convolved = jnp.zeros(sequence.shape, jnp.float32)
    for offset in range(CONV):
        convolved = convolved + conv_weight[offset] * padded[CONV - 1 - offset:CONV - 1 - offset + length]
    projected = rounded(convolved)
    blocks = length // BLOCK
    half = HEADS * HEAD // 2
    half_heads = HEADS // 2
    shape_four = (blocks, BLOCK, half_heads, HEAD)
    query_a = projected[:, 0:half].reshape(shape_four)
    key_b = projected[:, 3 * half:4 * half].reshape(shape_four)
    value_a = projected[:, 4 * half:5 * half].reshape(shape_four)
    value_b = projected[:, 5 * half:6 * half].reshape(shape_four)
    probe = out_cotangent.astype(jnp.float32)
    probe_a = probe[:, 0:half].reshape(shape_four)
    probe_b = probe[:, half:2 * half].reshape(shape_four)
    states = jnp.einsum('bshd,bshe->bhde', key_b, value_b)
    adjoints = jnp.einsum('bshd,bshe->bhde', query_a, probe_a)
    nothing = jnp.zeros_like(states[:1])
    before = jnp.concatenate([nothing, jnp.cumsum(states, 0)[:-1]], 0)
    following = jnp.concatenate([jnp.cumsum(adjoints[::-1], 0)[::-1][1:], nothing], 0)
    before_half = rounded(before)
    after_half = rounded(following)
    causal = jnp.tril(jnp.ones((BLOCK, BLOCK), jnp.bool_))
    scores_b = rounded(jnp.where(causal, jnp.einsum('bthd,bshd->bhts', probe_b, value_b) / HEAD, 0.0))
    scores_a = rounded(jnp.where(causal, jnp.einsum('bthd,bshd->bhts', probe_a, value_a) / HEAD, 0.0))
    query_grad = jnp.einsum('bhts,bshd->bthd', scores_b, key_b) + jnp.einsum('bthe,bhde->bthd', probe_b, before_half) / HEAD
    key_grad = jnp.einsum('bhts,bthd->bshd', scores_a, query_a) + jnp.einsum('bshe,bhde->bshd', value_a, after_half) / HEAD
    kept = jnp.concatenate([query_grad.reshape(length, half), key_grad.reshape(length, half)], 1)
    extended = jnp.pad(kept, ((0, CONV - 1), (0, 0)))
    input_grad = jnp.zeros((length, 2 * half), jnp.float32)
    for offset in range(CONV):
        input_grad = input_grad + conv_weight[offset, half:3 * half] * extended[offset:offset + length]
    weight_terms = jnp.stack([jnp.sum(kept * padded[CONV - 1 - offset:CONV - 1 - offset + length, half:3 * half], 0) for offset in range(CONV)], 0)
    return input_grad.astype(jnp.bfloat16), weight_terms


def reference(qkv_input, conv_weight, out_cotangent):
    input_grad, weight_terms = lax.map(lambda pair: one_sequence(pair[0], conv_weight, pair[1]), (qkv_input, out_cotangent))
    return input_grad, jnp.sum(weight_terms, 0) / SEQS
```

```python
import jax
import jax.numpy as jnp
from jax import lax
from jax.experimental import pallas as pl
from jax.experimental.pallas import tpu as pltpu
from jax.sharding import Mesh
from jax.sharding import PartitionSpec as P

HEAD = 128
TAPS = 4
ROWS = 128
PAIR = 2 * ROWS
EXT = PAIR + 16
PRE = 8
F32 = jnp.float32
BF16 = jnp.bfloat16
QA, QB, KA, KB, VA, VB, GA, GB = range(8)
VMEM = pl.BlockSpec(memory_space=pltpu.VMEM)
SMEM = pl.BlockSpec(memory_space=pltpu.SMEM)


def call(kernel, shapes, scratch, scalars, *arrays):
    return pl.pallas_call(
        kernel,
        out_shape=[jax.ShapeDtypeStruct(s, t) for s, t in shapes],
        in_specs=[SMEM] + [VMEM] * len(arrays),
        out_specs=[VMEM] * len(shapes),
        scratch_shapes=scratch,
        compiler_params=pltpu.CompilerParams(vmem_limit_bytes=32 * 1024 * 1024),
    )(scalars, *arrays)


def nt(a, b):
    return lax.dot_general(a, b, (((1,), (1,)), ((), ())), preferred_element_type=F32)


def tn(a, b):
    return lax.dot_general(a, b, (((0,), (0,)), ((), ())), preferred_element_type=F32)


def nn(a, b):
    return lax.dot_general(a, b, (((1,), (0,)), ((), ())), preferred_element_type=F32)


def own_columns(x_ref, g_ref, group, half, width):
    ref, at = (x_ref, group) if group < GA else (g_ref, group - GA)
    return ref, pl.ds(pl.multiple_of((2 * at + half) * width, HEAD), width)


def pack_kernel(scalars, x_ref, g_ref, send_ref, same_ref, cross_ref):
    core = scalars[0]
    width = same_ref.shape[1]
    edge = pl.ds(pl.multiple_of(core * (ROWS - 16), 16), 16)
    for half, out_ref in ((core, same_ref), (1 - core, cross_ref)):
        pieces = []
        for group in range(8):
            ref, lanes = own_columns(x_ref, g_ref, group, half, width)
            rows = ref[edge, lanes].astype(F32)
            pieces.append(jnp.where(core == 1, rows[12:16], rows[0:4]))
        out_ref[...] = jnp.concatenate(pieces, 0).astype(BF16)
    for group in range(8):
        ref, lanes = own_columns(x_ref, g_ref, group, 1 - core, width)
        send_ref[:, group * width : (group + 1) * width] = ref[:, lanes]


def edges(core, same_ref, cross_ref):
    same, cross = same_ref[...].astype(F32), cross_ref[...].astype(F32)
    return jnp.where(core == 1, same, cross), jnp.where(core == 1, cross, same)


def gather_rows(core, x_ref, g_ref, received_ref, group, head, padded_ref):
    width = received_ref.shape[1] // 8
    half_at = core * width + head * HEAD
    ref, at = (x_ref, group) if group < GA else (g_ref, group - GA)
    lanes = pl.ds(pl.multiple_of(2 * at * width + half_at, HEAD), HEAD)
    own = ref[:, lanes].astype(F32)
    other = received_ref[:, group * width + head * HEAD : group * width + (head + 1) * HEAD]
    padded_ref[pl.ds(pl.multiple_of(PRE + core * ROWS, 8), ROWS), :] = own
    padded_ref[pl.ds(pl.multiple_of(PRE + (1 - core) * ROWS, 8), ROWS), :] = other.astype(F32)


def fill_edges(before, after, group, head, padded_ref):
    lanes = slice(head * HEAD, (head + 1) * HEAD)
    none = jnp.zeros((4, HEAD), F32)
    rows = slice(4 * group, 4 * group + 4)
    padded_ref[0:PRE, :] = jnp.concatenate([none, before[rows, lanes]], 0)
    padded_ref[PRE + PAIR : PRE + PAIR + 8, :] = jnp.concatenate([after[rows, lanes], none], 0)


def convolve(padded_ref, w_ref, core, width, group, head, out_ref):
    lanes = pl.ds(pl.multiple_of((2 * group + core) * width + head * HEAD, HEAD), HEAD)
    taps = w_ref[:, lanes]
    at = slice(head * HEAD, (head + 1) * HEAD)
    for first, count in ((0, ROWS), (ROWS, ROWS), (PAIR, 8)):
        start = PRE + first
        total = taps[0:1] * padded_ref[start : start + count, :]
        for j in range(1, TAPS):
            total = total + taps[j : j + 1] * padded_ref[start - j : start - j + count, :]
        if first == PAIR:
            total = jnp.concatenate([total, jnp.zeros((8, HEAD), F32)], 0)
            count = 16
        out_ref[first : first + count, at] = total.astype(BF16)


def copy_rows(padded_ref, head, out_ref):
    at = slice(head * HEAD, (head + 1) * HEAD)
    out_ref[0:PAIR, at] = padded_ref[PRE : PRE + PAIR, :].astype(BF16)
    tail = padded_ref[PRE + PAIR : PRE + PAIR + 8, :]
    out_ref[PAIR:EXT, at] = jnp.concatenate([tail, jnp.zeros((8, HEAD), F32)], 0).astype(BF16)


def states_kernel(
    scalars, x_ref, g_ref, received_ref, same_ref, cross_ref, w_ref,
    up_ref, down_ref, far_ref, qa_ref, kb_ref, vb_ref, ga_ref, *padded_refs,
):
    core, chip = scalars[0], scalars[1]
    width = received_ref.shape[1] // 8
    before, after = edges(core, same_ref, cross_ref)
    turn = 0
    for head in range(width // HEAD):
        for group, out_ref in ((KB, kb_ref), (VB, vb_ref), (QA, qa_ref), (GA, ga_ref)):
            padded_ref = padded_refs[turn % len(padded_refs)]
            turn += 1
            gather_rows(core, x_ref, g_ref, received_ref, group, head, padded_ref)
            fill_edges(before, after, group, head, padded_ref)
            if group == GA:
                copy_rows(padded_ref, head, out_ref)
            else:
                convolve(padded_ref, w_ref, core, width, group, head, out_ref)
        at = slice(head * HEAD, (head + 1) * HEAD)
        state = tn(kb_ref[0:PAIR, at], vb_ref[0:PAIR, at]).astype(BF16)
        adjoint = tn(qa_ref[0:PAIR, at], ga_ref[0:PAIR, at]).astype(BF16)
        up_ref[head] = jnp.where(chip == 3, adjoint, state)
        down_ref[head] = jnp.where(chip == 0, state, adjoint)
        far_ref[head] = jnp.where(chip < 2, state, adjoint)


def inside_kernel(
    scalars, x_ref, g_ref, received_ref, same_ref, cross_ref, w_ref,
    qa_ref, kb_ref, vb_ref, ga_ref,
    kept_ref, va_ref, gb_ref, raw_ref, *padded_refs,
):
    core = scalars[0]
    width = received_ref.shape[1] // 8
    before, after = edges(core, same_ref, cross_ref)
    row = lax.broadcasted_iota(jnp.int32, (EXT, EXT), 0)
    column = lax.broadcasted_iota(jnp.int32, (EXT, EXT), 1)
    causal = jnp.where(column <= row, 1.0 / HEAD, 0.0)
    reverse = jnp.where(
        (column >= row) & (column < PAIR),
        1.0 / HEAD,
        jnp.where((column >= PAIR) & (column < row), -1.0 / HEAD, 0.0),
    )
    turn = 0
    for head in range(width // HEAD):
        at = slice(head * HEAD, (head + 1) * HEAD)
        for group in (VA, GB, QB, KA):
            padded_ref = padded_refs[turn % len(padded_refs)]
            turn += 1
            gather_rows(core, x_ref, g_ref, received_ref, group, head, padded_ref)
            fill_edges(before, after, group, head, padded_ref)
            if group == VA:
                convolve(padded_ref, w_ref, core, width, group, head, va_ref)
            elif group == GB:
                copy_rows(padded_ref, head, gb_ref)
            else:
                to = slice((group - QB) * width + head * HEAD, (group - QB) * width + (head + 1) * HEAD)
                raw_ref[:, to] = padded_ref[...]
        scores = (nt(gb_ref[:, at], vb_ref[:, at]) * causal).astype(BF16)
        kept_ref[:, at] = nn(scores, kb_ref[:, at])
        scores = (nt(va_ref[:, at], ga_ref[:, at]) * reverse).astype(BF16)
        kept_ref[:, width + head * HEAD : width + (head + 1) * HEAD] = nn(scores, qa_ref[:, at])


def gradients_kernel(
    scalars, kept_ref, va_ref, gb_ref, raw_ref, up_ref, down_ref, far_ref, w_ref,
    own_ref, send_ref, terms_ref, total_ref, grad_ref,
):
    core, chip = scalars[0], scalars[1]
    width = va_ref.shape[1]
    for head in range(width // HEAD):
        up, down, far = (r[head].astype(F32) for r in (up_ref, down_ref, far_ref))
        none = jnp.zeros_like(up)
        earlier = (
            jnp.where(chip >= 1, up, none) + jnp.where(chip >= 2, far, none)
            + jnp.where(chip == 3, down, none)
        ).astype(BF16)
        later = (
            jnp.where(chip <= 2, down, none) + jnp.where(chip <= 1, far, none)
            + jnp.where(chip == 0, up, none)
        ).astype(BF16)
        at = slice(head * HEAD, (head + 1) * HEAD)
        for part, left_ref, right in ((0, gb_ref, earlier), (1, va_ref, later)):
            to = slice(part * width + head * HEAD, part * width + (head + 1) * HEAD)
            total_ref[:, :] = kept_ref[:, to] + nt(left_ref[:, at], right) * (1.0 / HEAD)
            group = QB + part
            lanes = pl.ds(pl.multiple_of((2 * group + core) * width + head * HEAD, HEAD), HEAD)
            taps = w_ref[:, lanes]
            sums = [jnp.zeros((8, HEAD), F32)] * TAPS
            for first in range(0, PAIR, 64):
                grad = taps[0:1] * total_ref[first : first + 64, :]
                for j in range(1, TAPS):
                    grad = grad + taps[j : j + 1] * total_ref[first + j : first + j + 64, :]
                grad_ref[first : first + 64, to] = grad.astype(BF16)
                kept = total_ref[first : first + 64, :]
                for j in range(TAPS):
                    start = PRE + first - j
                    term = kept * raw_ref[start : start + 64, to]
                    sums[j] = sums[j] + jnp.sum(term.reshape(8, 8, HEAD), 0)
            terms_ref[:, to] = jnp.concatenate(
                [jnp.sum(s, 0, keepdims=True) for s in sums], 0
            )
    own_ref[...] = grad_ref[pl.ds(pl.multiple_of(core * ROWS, ROWS), ROWS), :]
    send_ref[...] = grad_ref[pl.ds(pl.multiple_of((1 - core) * ROWS, ROWS), ROWS), :]


def per_device(qkv_input, conv_weight, out_cotangent):
    x, g = qkv_input[0], out_cotangent[0]
    half = g.shape[1] // 2
    width = half // 2
    heads = width // HEAD
    chips = lax.axis_size("zh")
    core, chip, low = lax.axis_index("core"), lax.axis_index("zh"), lax.axis_index("zl")
    scalars = jnp.stack([core, chip]).astype(jnp.int32)
    swap = [(0, 1), (1, 0)]
    line = (("zh", "core"))

    def place(c, k):
        return 2 * c + k

    to_same = [(place(c, 1), place(c + 1, 1)) for c in range(chips - 1)]
    to_same += [(place(c + 1, 0), place(c, 0)) for c in range(chips - 1)]
    to_cross = [(place(c, 1), place(c + 1, 0)) for c in range(chips - 1)]
    to_cross += [(place(c + 1, 0), place(c, 1)) for c in range(chips - 1)]

    send, same, cross = call(
        pack_kernel,
        [((ROWS, 8 * width), BF16), ((32, width), BF16), ((32, width), BF16)],
        [], scalars, x, g,
    )
    received = lax.ppermute(send, "core", swap)
    same = lax.ppermute(same, line, to_same)
    cross = lax.ppermute(cross, line, to_cross)

    block = ((heads, HEAD, HEAD), BF16)
    long = ((EXT, width), BF16)
    padded = [pltpu.VMEM((PRE + PAIR + 8, HEAD), F32)] * 4
    up, down, far, qa, kb, vb, ga = call(
        states_kernel, [block] * 3 + [long] * 4, padded,
        scalars, x, g, received, same, cross, conv_weight,
    )
    far = lax.ppermute(far, "zh", [(c, (c + 2) % chips) for c in range(chips)])
    up = lax.ppermute(up, "zh", [(c, (c + 1) % chips) for c in range(chips)])
    down = lax.ppermute(down, "zh", [(c, (c - 1) % chips) for c in range(chips)])

    kept, va, gb, raw = call(
        inside_kernel,
        [((EXT, half), F32), long, long, ((PRE + PAIR + 8, half), F32)], padded,
        scalars, x, g, received, same, cross, conv_weight, qa, kb, vb, ga,
    )
    own, sent, terms = call(
        gradients_kernel,
        [((ROWS, half), BF16), ((ROWS, half), BF16), ((TAPS, half), F32)],
        [pltpu.VMEM((EXT, HEAD), F32), pltpu.VMEM((PAIR, half), BF16)],
        scalars, kept, va, gb, raw, up, down, far, conv_weight,
    )
    other = lax.ppermute(sent, "core", swap)

    spread = lax.axis_size("yx")
    few = width // spread
    rows = terms.reshape(TAPS, 2, spread, few).transpose(2, 1, 0, 3).reshape(spread, 2 * TAPS * few)
    summed = jnp.sum(lax.all_to_all(rows, "yx", 0, 0, tiled=True), 0).reshape(2, TAPS * few)
    along = 2 * chips
    rows = jnp.repeat(summed, 2 * along, axis=0)
    rows = lax.all_to_all(rows, ("zl", "zh", "core"), 0, 0, tiled=True)
    fitting = (jnp.arange(4 * along) % 2 == low % 2)[:, None]
    share = jnp.sum(jnp.where(fitting, rows, 0.0), 0).reshape(TAPS, few)
    shares = share / (lax.axis_size("zl") * spread)

    first, second = jnp.where(core == 0, own, other), jnp.where(core == 0, other, own)
    grad = jnp.concatenate(
        [first[:, :width], second[:, :width], first[:, width:], second[:, width:]], 1
    )
    return grad[None], shares


def solution(mesh):
    dp, seq = mesh.shape["dp"], mesh.shape["seq"]
    fine = Mesh(mesh.devices.reshape(4, dp // 4, seq // 2, 2), ("zl", "yx", "zh", "core"))
    rows = P(("zl", "yx"), ("zh", "core"), None)
    return jax.shard_map(
        per_device, mesh=fine, in_specs=(rows, P(), rows),
        out_specs=(rows, P(None, ("zl", "yx"))), check_vma=False,
    )
```

```python
import jax
import jax.numpy as jnp
from jax import lax
from jax.experimental import pallas as pl
from jax.experimental.pallas import tpu as pltpu
from jax.sharding import Mesh
from jax.sharding import PartitionSpec as P

HEAD = 128
TAPS = 4
ROWS = 128
PAIR = 2 * ROWS
EXT = PAIR + 16
PRE = 8
LONG = PRE + PAIR + 8
EDGE = 8
F32 = jnp.float32
BF16 = jnp.bfloat16
LEFT, A, B, RAW = range(4)
VMEM = pl.BlockSpec(memory_space=pltpu.VMEM)
SMEM = pl.BlockSpec(memory_space=pltpu.SMEM)


def call(kernel, shapes, scratch, scalars, *arrays, space=VMEM, limit=32):
    return pl.pallas_call(
        kernel,
        out_shape=[jax.ShapeDtypeStruct(s, t) for s, t in shapes],
        in_specs=[SMEM] + [space] * len(arrays),
        out_specs=[VMEM] * len(shapes),
        scratch_shapes=scratch,
        compiler_params=pltpu.CompilerParams(vmem_limit_bytes=limit * 1024 * 1024),
    )(scalars, *arrays)


def nt(a, b):
    return lax.dot_general(a, b, (((1,), (1,)), ((), ())), preferred_element_type=F32)


def tn(a, b):
    return lax.dot_general(a, b, (((0,), (0,)), ((), ())), preferred_element_type=F32)


def nn(a, b):
    return lax.dot_general(a, b, (((1,), (0,)), ((), ())), preferred_element_type=F32)


def lanes(group, head, width):
    return slice(group * width + head * HEAD, group * width + (head + 1) * HEAD)


def pack_kernel(scalars, x_ref, g_ref, keep_ref, send_ref, sems):
    core = scalars[0]
    width = keep_ref.shape[1] // 4
    of_core = (
        ((x_ref, 3), (g_ref, 1), (x_ref, 5), (x_ref, 1)),
        ((x_ref, 0), (x_ref, 4), (g_ref, 0), (x_ref, 2)),
    )

    def fill(mine):
        copies = []

        def copy(source_ref, group, out_ref, slot):
            lanes_in = slice(group * width, (group + 1) * width)
            lanes_out = slice(slot * width, (slot + 1) * width)
            copies.append(
                pltpu.make_async_copy(
                    source_ref.at[:, lanes_in], out_ref.at[:, lanes_out], sems.at[len(copies)]
                )
            )

        for slot, (source_ref, group) in enumerate(of_core[1 - mine]):
            copy(source_ref, group, send_ref, slot)
        for slot, (source_ref, group) in enumerate(of_core[mine]):
            copy(source_ref, group, keep_ref, slot)
        for each in copies:
            each.start()
        for each in copies:
            each.wait()

    @pl.when(core == 0)
    def _():
        fill(0)

    @pl.when(core == 1)
    def _():
        fill(1)


def taps_kernel(scalars, w_ref, taps_ref):
    width = taps_ref.shape[1] // 4
    row = lax.broadcasted_iota(jnp.int32, (TAPS, width), 0)
    unit = jnp.where(row == 0, 1.0, 0.0).astype(F32)
    for core, groups in enumerate(((3, None, 5, 1), (0, 4, None, 2))):

        @pl.when(scalars[0] == core)
        def _():
            for slot, group in enumerate(groups):
                part = unit if group is None else w_ref[:, group * width : (group + 1) * width]
                taps_ref[:, slot * width : (slot + 1) * width] = part


def gather_rows(core, keep_ref, received_ref, at, padded_ref):
    own = pl.ds(pl.multiple_of(PRE + core * ROWS, 8), ROWS)
    other = pl.ds(pl.multiple_of(PRE + (1 - core) * ROWS, 8), ROWS)
    padded_ref[own, :] = keep_ref[:, at].astype(F32)
    padded_ref[other, :] = received_ref[:, at].astype(F32)


def convolved(padded_ref, taps, start, count):
    total = taps[0:1] * padded_ref[start : start + count, :]
    for j in range(1, TAPS):
        total = total + taps[j : j + 1] * padded_ref[start - j : start - j + count, :]
    return total


def states_kernel(scalars, keep_ref, received_ref, taps_ref, message_ref, wrap_ref, *scratch):
    core, chip = scalars[0], scalars[1]
    width = keep_ref.shape[1] // 4
    padded_refs, value_refs = scratch[:4], scratch[4:]
    for ref in padded_refs:
        ref[0:PRE, :] = jnp.zeros((PRE, HEAD), F32)
    row = lax.broadcasted_iota(jnp.int32, (ROWS, HEAD), 0)
    kept_rows = (row >= TAPS - 1) | (chip == 0)
    first_rows = jnp.where(chip == 0, 0.0, 1.0)
    for head in range(width // HEAD):
        firsts, lasts = [], []
        for turn, group in enumerate((LEFT, B)):
            padded_ref = padded_refs[(2 * head + turn) % 4]
            value_ref = value_refs[(2 * head + turn) % 4]
            at = lanes(group, head, width)
            gather_rows(core, keep_ref, received_ref, at, padded_ref)
            taps = taps_ref[:, at]
            for first in (0, ROWS):
                total = convolved(padded_ref, taps, PRE + first, ROWS)
                if group == LEFT and first == 0:
                    total = jnp.where(kept_rows, total, 0.0)
                value_ref[first : first + ROWS, :] = total.astype(BF16)
            front = padded_ref[PRE : PRE + 4, :]
            firsts.append(front * first_rows if group == LEFT else front)
            lasts.append(padded_ref[PRE + PAIR - 4 : PRE + PAIR, :])
        left, right = value_refs[(2 * head) % 4], value_refs[(2 * head + 1) % 4]
        state = tn(left[...], right[...]).astype(BF16)
        firsts, lasts = jnp.concatenate(firsts, 0), jnp.concatenate(lasts, 0)
        for ref in (message_ref, wrap_ref):
            ref[head, 0:HEAD, :] = state
        message_ref[head, HEAD:, :] = jnp.concatenate([firsts, lasts], 0).astype(BF16)
        wrap_ref[head, HEAD:, :] = jnp.where(core == 0, lasts, firsts).astype(BF16)


def edge_rows_kernel(scalars, keep_ref, send_ref, message_ref, same_ref, cross_ref):
    core = scalars[0]
    width = keep_ref.shape[1] // 4
    edge = pl.ds(pl.multiple_of(core * (ROWS - 16), 16), 16)
    for ref, out_ref, later in ((keep_ref, same_ref, A), (send_ref, cross_ref, B)):
        for slot, (first, last) in enumerate(((LEFT, LEFT), (A, later), (B, RAW))):
            zero = ref[edge, first * width : (first + 1) * width].astype(F32)[0:4]
            one = ref[edge, last * width : (last + 1) * width].astype(F32)[12:16]
            rows = jnp.where(core == 1, one, zero).astype(BF16)
            out_ref[:, slot * width : (slot + 1) * width] = rows


def inside_kernel(
    scalars, keep_ref, received_ref, same_ref, cross_ref, taps_ref,
    kept_ref, a_ref, raw_ref, left_tail_ref, b_tail_ref, *scratch,
):
    core = scalars[0]
    width = keep_ref.shape[1] // 4
    padded_refs, value_refs = scratch[:4], scratch[4:]
    same, cross = same_ref[...].astype(F32), cross_ref[...].astype(F32)
    before, after = jnp.where(core == 1, same, cross), jnp.where(core == 1, cross, same)
    row = lax.broadcasted_iota(jnp.int32, (EXT, EXT), 0)
    column = lax.broadcasted_iota(jnp.int32, (EXT, EXT), 1)
    causal = jnp.where(column <= row, 1.0 / HEAD, 0.0)
    reverse = jnp.where(
        (column >= row) & (column < PAIR),
        1.0 / HEAD,
        jnp.where((column >= PAIR) & (column < row), -1.0 / HEAD, 0.0),
    )
    mask = jnp.where(core == 0, causal, reverse)
    none = jnp.zeros((4, HEAD), F32)
    tail_row = lax.broadcasted_iota(jnp.int32, (16, HEAD), 0)
    tail_used = (tail_row < TAPS - 1) & (core == 1)
    turn = 0
    for head in range(width // HEAD):
        to = lanes(0, head, width)
        values = []
        for group in (LEFT, A, B, RAW):
            padded_ref = padded_refs[turn % 4]
            value_ref = value_refs[turn % 4]
            turn += 1
            at = lanes(group, head, width)
            gather_rows(core, keep_ref, received_ref, at, padded_ref)
            front = before[:, lanes((0, 1, 1, 2)[group], head, width)]
            back = after[:, lanes((0, 1, 2, 2)[group], head, width)]
            padded_ref[0:PRE, :] = jnp.concatenate([none, front], 0)
            padded_ref[PRE + PAIR : LONG, :] = jnp.concatenate([back, none], 0)
            if group == RAW:
                raw_ref[:, to] = padded_ref[...]
                continue
            taps = taps_ref[:, at]
            for first in (0, ROWS):
                total = convolved(padded_ref, taps, PRE + first, ROWS)
                value_ref[first : first + ROWS, :] = total.astype(BF16)
            tail = convolved(padded_ref, taps, PRE + PAIR, 8)
            tail = jnp.concatenate([tail, jnp.zeros((8, HEAD), F32)], 0)
            value_ref[PAIR:EXT, :] = tail.astype(BF16)
            if group != A:
                tail_ref = left_tail_ref if group == LEFT else b_tail_ref
                tail_ref[:, to] = jnp.where(tail_used, tail, 0.0).astype(BF16)
            values.append(value_ref)
        left, a, b = (ref[...] for ref in values)
        a_ref[:, to] = a
        scores = (nt(a, b) * mask).astype(BF16)
        kept_ref[:, to] = nn(scores, left)


def kept_kernel(
    scalars, inside_ref, a_ref, raw_ref, left_tail_ref, b_tail_ref, near_ref, far_ref, wrap_ref,
    taps_ref, kept_ref, terms_ref, edge_ref,
):
    core = scalars[0]
    width = a_ref.shape[1]
    row = lax.broadcasted_iota(jnp.int32, (8, HEAD), 0)
    nothing = jnp.zeros((8, HEAD), F32)
    for head in range(width // HEAD):
        to = lanes(0, head, width)
        near, far, wrap = (r[head, HEAD:, :].astype(F32) for r in (near_ref, far_ref, wrap_ref))
        near = jnp.where(core == 0, near[0:EDGE], near[EDGE : 2 * EDGE])
        first, last = far[0:EDGE], far[EDGE : 2 * EDGE]
        rows = []
        seams = []
        for zero, one in (((last, near), (near, first)), ((wrap, first), (last, wrap))):
            seams.append([jnp.where(core == 0, *pair) for pair in zip(zero, one)])
        for group, at in ((LEFT, slice(0, 4)), (B, slice(4, 8))):
            taps = taps_ref[:, lanes(group, head, width)]
            for turn, seam in enumerate(seams):
                part = edge_ref.at[2 * (group // 2) + turn]
                part[0:8, :] = jnp.concatenate([seam[0][at], seam[1][at]], 0)
                part[8:16, :] = nothing
                total = convolved(part, taps, 4, 8)
                rows.append(jnp.where(row < TAPS - 1, total, 0.0))
        left = jnp.concatenate(rows[0:2], 0).astype(BF16)
        right = jnp.concatenate(rows[2:4], 0).astype(BF16)
        state = (
            near_ref[head, 0:HEAD, :].astype(F32) + far_ref[head, 0:HEAD, :].astype(F32)
            + wrap_ref[head, 0:HEAD, :].astype(F32)
            + tn(left, right) + tn(left_tail_ref[:, to], b_tail_ref[:, to])
        ).astype(BF16)
        kept_ref[:, to] = inside_ref[:, to] + nt(a_ref[:, to], state) * (1.0 / HEAD)
        sums = [jnp.zeros((8, HEAD), F32)] * TAPS
        for first in range(0, PAIR, 64):
            kept = kept_ref[first : first + 64, to]
            for j in range(TAPS):
                start = PRE + first - j
                term = kept * raw_ref[start : start + 64, to]
                sums[j] = sums[j] + jnp.sum(term.reshape(8, 8, HEAD), 0)
        terms_ref[:, to] = jnp.concatenate([jnp.sum(s, 0, keepdims=True) for s in sums], 0)


def input_kernel(scalars, kept_ref, taps_ref, own_ref, send_ref, grad_ref):
    core = scalars[0]
    width = own_ref.shape[1]
    for head in range(width // HEAD):
        to = lanes(0, head, width)
        taps = taps_ref[:, lanes(RAW, head, width)]
        for first in range(0, PAIR, 64):
            grad = taps[0:1] * kept_ref[first : first + 64, to]
            for j in range(1, TAPS):
                grad = grad + taps[j : j + 1] * kept_ref[first + j : first + j + 64, to]
            grad_ref[first : first + 64, to] = grad.astype(BF16)
    own_ref[...] = grad_ref[pl.ds(pl.multiple_of(core * ROWS, ROWS), ROWS), :]
    send_ref[...] = grad_ref[pl.ds(pl.multiple_of((1 - core) * ROWS, ROWS), ROWS), :]


def per_device(qkv_input, conv_weight, out_cotangent):
    x, g = qkv_input[0], out_cotangent[0]
    width = g.shape[1] // 2
    heads = width // HEAD
    chips = lax.axis_size("zh")
    core, chip, low = lax.axis_index("core"), lax.axis_index("zh"), lax.axis_index("zl")
    scalars = jnp.stack([core, chip]).astype(jnp.int32)
    swap = [(0, 1), (1, 0)]
    line = ("zh", "core")

    def hops(by):
        later = [(2 * c, 2 * (c + by)) for c in range(chips - by)]
        return later + [(2 * (c + by) + 1, 2 * c + 1) for c in range(chips - by)]

    pairs = range(chips - 1)
    to_same = [(2 * c + 1, 2 * c + 3) for c in pairs] + [(2 * c + 2, 2 * c) for c in pairs]
    to_cross = [(2 * c + 1, 2 * c + 2) for c in pairs] + [(2 * c + 2, 2 * c + 1) for c in pairs]

    keep, send = call(
        pack_kernel, [((ROWS, 4 * width), BF16)] * 2, [pltpu.SemaphoreType.DMA((8,))],
        scalars, x, g, space=pl.BlockSpec(memory_space=pl.ANY), limit=8,
    )
    (taps,) = call(taps_kernel, [((TAPS, 4 * width), F32)], [], scalars, conv_weight)
    received = lax.ppermute(send, "core", swap)
    padded = [pltpu.VMEM((LONG, HEAD), F32)] * 4
    message, wrap = call(
        states_kernel,
        [((heads, HEAD + size, HEAD), BF16) for size in (2 * EDGE, EDGE)],
        padded + [pltpu.VMEM((PAIR, HEAD), BF16)] * 4,
        scalars, keep, received, taps,
    )
    same, cross = call(
        edge_rows_kernel, [((4, 3 * width), BF16)] * 2, [], scalars, keep, send, message
    )
    near = lax.ppermute(message, line, hops(1))
    far = lax.ppermute(message, line, hops(2))
    wrap = lax.ppermute(wrap, line, hops(3))
    same = lax.ppermute(same, line, to_same)
    cross = lax.ppermute(cross, line, to_cross)
    inside, a, raw, left_tail, b_tail = call(
        inside_kernel,
        [((EXT, width), F32), ((EXT, width), BF16), ((LONG, width), F32)]
        + [((16, width), BF16)] * 2,
        padded + [pltpu.VMEM((EXT, HEAD), BF16)] * 4,
        scalars, keep, received, same, cross, taps,
    )
    kept, terms = call(
        kept_kernel, [((EXT, width), F32), ((TAPS, width), F32)],
        [pltpu.VMEM((4, 16, HEAD), F32)],
        scalars, inside, a, raw, left_tail, b_tail, near, far, wrap, taps,
    )

    spread = lax.axis_size("yx")
    few = width // 2 // spread
    rows = terms.reshape(TAPS, 2, spread, few).transpose(2, 1, 0, 3).reshape(spread, 2 * TAPS * few)
    summed = jnp.sum(lax.all_to_all(rows, "yx", 0, 0, tiled=True), 0).reshape(2, TAPS * few)
    rows = jnp.broadcast_to(summed[None, None, :, None], (2, 2, 2, chips, TAPS * few))
    rows = lax.all_to_all(
        rows.reshape(8 * chips, TAPS * few), ("core", "zl", "zh"), 0, 0, tiled=True
    )
    fitting = (jnp.arange(8 * chips) // (4 * chips) == low // 2)[:, None]
    share = jnp.sum(jnp.where(fitting, rows, 0.0), 0).reshape(TAPS, few)
    shares = share / (lax.axis_size("zl") * spread)

    own, sent = call(
        input_kernel, [((ROWS, width), BF16)] * 2, [pltpu.VMEM((PAIR, width), BF16)],
        scalars, kept, taps,
    )
    other = lax.ppermute(sent, "core", swap)
    first, second = jnp.where(core == 0, own, other), jnp.where(core == 0, other, own)
    return jnp.concatenate([first, second], 1)[None], shares


def solution(mesh):
    dp, seq = mesh.shape["dp"], mesh.shape["seq"]
    fine = Mesh(mesh.devices.reshape(4, dp // 4, seq // 2, 2), ("zl", "yx", "zh", "core"))
    rows = P(("zl", "yx"), ("zh", "core"), None)
    return jax.shard_map(
        per_device, mesh=fine, in_specs=(rows, P(), rows),
        out_specs=(rows, P(None, ("zl", "yx"))), check_vma=False,
    )
```

```python
import jax
import jax.numpy as jnp
from jax import lax
from jax.experimental import pallas as pl
from jax.experimental.pallas import tpu as pltpu
from jax.sharding import Mesh
from jax.sharding import PartitionSpec as P

HEAD = 128
TAPS = 4
ROWS = 128
PAIR = 2 * ROWS
EXT = PAIR + 16
PRE = 8
LONG = PRE + PAIR + 8
EDGE = 8
F32 = jnp.float32
BF16 = jnp.bfloat16
LEFT, A, B, RAW = range(4)
VMEM = pl.BlockSpec(memory_space=pltpu.VMEM)
SMEM = pl.BlockSpec(memory_space=pltpu.SMEM)


def call(kernel, shapes, scratch, scalars, *arrays, space=VMEM, limit=32):
    return pl.pallas_call(
        kernel,
        out_shape=[jax.ShapeDtypeStruct(s, t) for s, t in shapes],
        in_specs=[SMEM] + [space] * len(arrays),
        out_specs=[VMEM] * len(shapes),
        scratch_shapes=scratch,
        compiler_params=pltpu.CompilerParams(vmem_limit_bytes=limit * 1024 * 1024),
    )(scalars, *arrays)


def nt(a, b):
    return lax.dot_general(a, b, (((1,), (1,)), ((), ())), preferred_element_type=F32)


def tn(a, b):
    return lax.dot_general(a, b, (((0,), (0,)), ((), ())), preferred_element_type=F32)


def nn(a, b):
    return lax.dot_general(a, b, (((1,), (0,)), ((), ())), preferred_element_type=F32)


def lanes(group, head, width):
    return slice(group * width + head * HEAD, group * width + (head + 1) * HEAD)


def pack_kernel(scalars, x_ref, g_ref, keep_ref, send_ref, sems):
    core = scalars[0]
    width = keep_ref.shape[1] // 4
    of_core = (
        ((x_ref, 3), (g_ref, 1), (x_ref, 5), (x_ref, 1)),
        ((x_ref, 0), (x_ref, 4), (g_ref, 0), (x_ref, 2)),
    )

    def fill(mine):
        copies = []

        def copy(source_ref, group, out_ref, slot):
            lanes_in = slice(group * width, (group + 1) * width)
            lanes_out = slice(slot * width, (slot + 1) * width)
            copies.append(
                pltpu.make_async_copy(
                    source_ref.at[:, lanes_in], out_ref.at[:, lanes_out], sems.at[len(copies)]
                )
            )

        for slot, (source_ref, group) in enumerate(of_core[1 - mine]):
            copy(source_ref, group, send_ref, slot)
        for slot, (source_ref, group) in enumerate(of_core[mine]):
            copy(source_ref, group, keep_ref, slot)
        for each in copies:
            each.start()
        for each in copies:
            each.wait()

    @pl.when(core == 0)
    def _():
        fill(0)

    @pl.when(core == 1)
    def _():
        fill(1)


def taps_kernel(scalars, w_ref, fitting_ref, taps_ref):
    width = taps_ref.shape[1] // 4
    row = lax.broadcasted_iota(jnp.int32, (TAPS, width), 0)
    unit = jnp.where(row == 0, 1.0, 0.0).astype(F32)
    for core, groups in enumerate(((3, None, 5, 1), (0, 4, None, 2))):

        @pl.when(scalars[0] == core)
        def _():
            for slot, group in enumerate(groups):
                part = unit if group is None else w_ref[:, group * width : (group + 1) * width]
                taps_ref[:, slot * width : (slot + 1) * width] = part


def gather_rows(core, keep_ref, received_ref, at, padded_ref):
    own = pl.ds(pl.multiple_of(PRE + core * ROWS, 8), ROWS)
    other = pl.ds(pl.multiple_of(PRE + (1 - core) * ROWS, 8), ROWS)
    padded_ref[own, :] = keep_ref[:, at].astype(F32)
    padded_ref[other, :] = received_ref[:, at].astype(F32)


def convolved(padded_ref, taps, start, count):
    total = taps[0:1] * padded_ref[start : start + count, :]
    for j in range(1, TAPS):
        total = total + taps[j : j + 1] * padded_ref[start - j : start - j + count, :]
    return total


def states_kernel(scalars, keep_ref, received_ref, taps_ref, message_ref, wrap_ref, *scratch):
    core, chip = scalars[0], scalars[1]
    width = keep_ref.shape[1] // 4
    padded_refs, value_refs = scratch[:4], scratch[4:]
    for ref in padded_refs:
        ref[0:PRE, :] = jnp.zeros((PRE, HEAD), F32)
    row = lax.broadcasted_iota(jnp.int32, (ROWS, HEAD), 0)
    kept_rows = (row >= TAPS - 1) | (chip == 0)
    first_rows = jnp.where(chip == 0, 0.0, 1.0)
    for head in range(width // HEAD):
        firsts, lasts = [], []
        for turn, group in enumerate((LEFT, B)):
            padded_ref = padded_refs[(2 * head + turn) % 4]
            value_ref = value_refs[(2 * head + turn) % 4]
            at = lanes(group, head, width)
            gather_rows(core, keep_ref, received_ref, at, padded_ref)
            taps = taps_ref[:, at]
            for first in (0, ROWS):
                total = convolved(padded_ref, taps, PRE + first, ROWS)
                if group == LEFT and first == 0:
                    total = jnp.where(kept_rows, total, 0.0)
                value_ref[first : first + ROWS, :] = total.astype(BF16)
            front = padded_ref[PRE : PRE + 4, :]
            firsts.append(front * first_rows if group == LEFT else front)
            lasts.append(padded_ref[PRE + PAIR - 4 : PRE + PAIR, :])
        left, right = value_refs[(2 * head) % 4], value_refs[(2 * head + 1) % 4]
        state = tn(right[...], left[...]).astype(BF16)
        firsts, lasts = jnp.concatenate(firsts, 0), jnp.concatenate(lasts, 0)
        for ref in (message_ref, wrap_ref):
            ref[head, 0:HEAD, :] = state
        message_ref[head, HEAD:, :] = jnp.concatenate([firsts, lasts], 0).astype(BF16)
        wrap_ref[head, HEAD:, :] = jnp.where(core == 0, lasts, firsts).astype(BF16)


def edge_rows_kernel(scalars, keep_ref, send_ref, message_ref, same_ref, cross_ref):
    core = scalars[0]
    width = keep_ref.shape[1] // 4
    edge = pl.ds(pl.multiple_of(core * (ROWS - 16), 16), 16)
    for ref, out_ref, later in ((keep_ref, same_ref, A), (send_ref, cross_ref, B)):
        for slot, (first, last) in enumerate(((LEFT, LEFT), (A, later), (B, RAW))):
            zero = ref[edge, first * width : (first + 1) * width].astype(F32)[0:4]
            one = ref[edge, last * width : (last + 1) * width].astype(F32)[12:16]
            rows = jnp.where(core == 1, one, zero).astype(BF16)
            out_ref[:, slot * width : (slot + 1) * width] = rows


def products_kernel(
    scalars, keep_ref, received_ref, taps_ref, after_ref, products_ref, fold_ref, rows_ref, *padded_refs
):
    core = scalars[0]
    width = keep_ref.shape[1] // 4
    for ref in padded_refs:
        ref[0:PRE, :] = jnp.zeros((PRE, HEAD), F32)
    row = lax.broadcasted_iota(jnp.int32, (PAIR, HEAD), 0)
    for head in range(width // HEAD):
        a_ref, raw_ref = (padded_refs[(2 * head + k) % 4] for k in range(2))
        at = lanes(A, head, width)
        gather_rows(core, keep_ref, received_ref, at, a_ref)
        gather_rows(core, keep_ref, received_ref, lanes(RAW, head, width), raw_ref)
        a = convolved(a_ref, taps_ref[:, at], PRE, PAIR)
        a = jnp.where(row >= TAPS - 1, a, 0.0).astype(BF16)
        for j in range(TAPS):
            shifted = raw_ref[PRE - j : PRE - j + PAIR, :].astype(BF16)
            products_ref[head, j] = tn(a, shifted) * (1.0 / HEAD)
    few = width // 2 // rows_ref.shape[0]
    place = lax.broadcasted_iota(jnp.int32, fold_ref.shape, 1)
    column = lax.broadcasted_iota(jnp.int32, fold_ref.shape, 0)
    place = lax.rem(place, fold_ref.shape[1] // 2)
    fits = (lax.rem(column, few) == lax.rem(place, few)) & (place < TAPS * few)
    fold_ref[...] = jnp.where(fits, 1.0, 0.0).astype(BF16)
    device = lax.broadcasted_iota(jnp.int32, rows_ref.shape, 0) * few
    column = lax.broadcasted_iota(jnp.int32, rows_ref.shape, 1)
    rows_ref[...] = jnp.where((column >= device) & (column < device + few), 1.0, 0.0)


def inside_kernel(
    scalars, keep_ref, received_ref, same_ref, cross_ref, taps_ref,
    kept_ref, a_ref, left_tail_ref, b_tail_ref, terms_ref, front_ref, *scratch,
):
    core = scalars[0]
    width = keep_ref.shape[1] // 4
    padded_refs, value_refs = scratch[:4], scratch[4:]
    same, cross = same_ref[...].astype(F32), cross_ref[...].astype(F32)
    before, after = jnp.where(core == 1, same, cross), jnp.where(core == 1, cross, same)
    row = lax.broadcasted_iota(jnp.int32, (EXT, EXT), 0)
    column = lax.broadcasted_iota(jnp.int32, (EXT, EXT), 1)
    causal = jnp.where(column <= row, 1.0 / HEAD, 0.0)
    reverse = jnp.where(
        (column >= row) & (column < PAIR),
        1.0 / HEAD,
        jnp.where((column >= PAIR) & (column < row), -1.0 / HEAD, 0.0),
    )
    mask = jnp.where(core == 0, causal, reverse)
    none = jnp.zeros((4, HEAD), F32)
    tail_row = lax.broadcasted_iota(jnp.int32, (16, HEAD), 0)
    tail_used = (tail_row < TAPS - 1) & (core == 1)
    turn = 0
    for head in range(width // HEAD):
        to = lanes(0, head, width)
        values = []
        for group in (LEFT, A, B, RAW):
            padded_ref = padded_refs[turn % 4]
            value_ref = value_refs[turn % 4]
            turn += 1
            at = lanes(group, head, width)
            gather_rows(core, keep_ref, received_ref, at, padded_ref)
            front = before[:, lanes((0, 1, 1, 2)[group], head, width)]
            back = after[:, lanes((0, 1, 2, 2)[group], head, width)]
            padded_ref[0:PRE, :] = jnp.concatenate([none, front], 0)
            padded_ref[PRE + PAIR : LONG, :] = jnp.concatenate([back, none], 0)
            if group == RAW:
                raw_ref = padded_ref
                continue
            taps = taps_ref[:, at]
            for first in (0, ROWS):
                total = convolved(padded_ref, taps, PRE + first, ROWS)
                value_ref[first : first + ROWS, :] = total.astype(BF16)
            tail = convolved(padded_ref, taps, PRE + PAIR, 8)
            tail = jnp.concatenate([tail, jnp.zeros((8, HEAD), F32)], 0)
            value_ref[PAIR:EXT, :] = tail.astype(BF16)
            if group != A:
                tail_ref = left_tail_ref if group == LEFT else b_tail_ref
                tail_ref[:, to] = jnp.where(tail_used, tail, 0.0).astype(BF16)
            values.append(value_ref)
        left, a, b = (ref[...] for ref in values)
        a_ref[:, to] = a
        scores = (nt(a, b) * mask).astype(BF16)
        kept_ref[:, to] = nn(scores, left)
        front_ref[:, to] = raw_ref[0 : PRE + 8, :]
        sums = [jnp.zeros((8, HEAD), F32)] * TAPS
        for first in range(0, PAIR, 64):
            kept = kept_ref[first : first + 64, to]
            for j in range(TAPS):
                start = PRE + first - j
                term = kept * raw_ref[start : start + 64, :]
                sums[j] = sums[j] + jnp.sum(term.reshape(8, 8, HEAD), 0)
        terms_ref[:, to] = jnp.concatenate([jnp.sum(s, 0, keepdims=True) for s in sums], 0)


def terms_kernel(
    scalars, terms_ref, products_ref, a_ref, front_ref, left_tail_ref, b_tail_ref,
    near_ref, far_ref, wrap_ref, taps_ref, fold_ref, rows_ref,
    states_ref, shares_ref, edge_ref, seam_ref, total_ref, stack_ref,
):
    core = scalars[0]
    heads, width = products_ref.shape[0], terms_ref.shape[1]
    none = jnp.zeros((8, HEAD), F32)
    for head in range(heads):
        to = lanes(0, head, width)
        near, far, wrap = (r[head, HEAD:, :].astype(F32) for r in (near_ref, far_ref, wrap_ref))
        near = jnp.where(core == 0, near[0:EDGE], near[EDGE : 2 * EDGE])
        first, last = far[0:EDGE], far[EDGE : 2 * EDGE]
        for turn, (zero, one) in enumerate((((last, near), (near, first)), ((wrap, first), (last, wrap)))):
            before, after = (jnp.where(core == 0, *pair) for pair in zip(zero, one))
            for slot, at in enumerate((slice(0, 4), slice(4, 8))):
                edge_ref[2 * slot + turn, 0:8, to] = jnp.concatenate([before[at], after[at]], 0)
                edge_ref[2 * slot + turn, 8:16, to] = none
    row = lax.broadcasted_iota(jnp.int32, (8, width), 0)
    for slot, group in enumerate((LEFT, B)):
        taps = taps_ref[:, group * width : (group + 1) * width]
        rows = [convolved(edge_ref.at[2 * slot + turn], taps, 4, 8) for turn in range(2)]
        rows = [jnp.where(row < TAPS - 1, total, 0.0) for total in rows]
        seam_ref[slot] = jnp.concatenate(rows, 0).astype(BF16)
    row = lax.broadcasted_iota(jnp.int32, (8, HEAD), 0)
    for head in range(heads):
        to = lanes(0, head, width)
        state = (
            near_ref[head, 0:HEAD, :].astype(F32) + far_ref[head, 0:HEAD, :].astype(F32)
            + wrap_ref[head, 0:HEAD, :].astype(F32)
            + tn(seam_ref[1, :, to], seam_ref[0, :, to])
            + tn(b_tail_ref[:, to], left_tail_ref[:, to])
        ).astype(BF16)
        states_ref[head] = state
        front = nn(a_ref[0:16, to], state)[0:8] * (1.0 / HEAD)
        front = jnp.where(row < TAPS - 1, front, 0.0)
        state = state.astype(F32)
        sums = []
        for j in range(TAPS):
            product = (state * products_ref[head, j]).reshape(HEAD // 8, 8, HEAD)
            total = jnp.sum(product, 0) + front * front_ref[PRE - j : PRE - j + 8, to]
            sums.append(jnp.sum(total, 0, keepdims=True))
        total_ref[:, to] = terms_ref[:, to] + jnp.concatenate(sums, 0)
    half = width // 2
    spread = rows_ref.shape[0]
    fitting = rows_ref[...]
    for part in range(2):
        for j in range(TAPS):
            at = (part * TAPS + j) * spread
            line = total_ref[j : j + 1, part * half : (part + 1) * half]
            stack_ref[at : at + spread, :] = fitting * line
    folded = nn(stack_ref[...].astype(BF16), fold_ref[...])
    few = half // spread
    place = lax.broadcasted_iota(jnp.int32, (spread, fold_ref.shape[1]), 1)
    gathered = jnp.zeros((spread, fold_ref.shape[1]), F32)
    for part in range(2):
        for j in range(TAPS):
            at = (part * TAPS + j) * spread
            begin = part * (fold_ref.shape[1] // 2) + j * few
            here = (place >= begin) & (place < begin + few)
            gathered = gathered + jnp.where(here, folded[at : at + spread], 0.0)
    shares_ref[...] = gathered.reshape(shares_ref.shape)


def input_kernel(
    scalars, inside_ref, a_ref, states_ref, taps_ref, after_ref, own_ref, send_ref, grad_ref, kept_ref
):
    core = scalars[0]
    width = own_ref.shape[1]
    for head in range(width // HEAD):
        to = lanes(0, head, width)
        kept_ref[:, to] = inside_ref[:, to] + nn(a_ref[:, to], states_ref[head]) * (1.0 / HEAD)
        taps = taps_ref[:, lanes(RAW, head, width)]
        for first in range(0, PAIR, 64):
            grad = taps[0:1] * kept_ref[first : first + 64, to]
            for j in range(1, TAPS):
                grad = grad + taps[j : j + 1] * kept_ref[first + j : first + j + 64, to]
            grad_ref[first : first + 64, to] = grad.astype(BF16)
    own_ref[...] = grad_ref[pl.ds(pl.multiple_of(core * ROWS, ROWS), ROWS), :]
    send_ref[...] = grad_ref[pl.ds(pl.multiple_of((1 - core) * ROWS, ROWS), ROWS), :]


def per_device(qkv_input, conv_weight, out_cotangent):
    x, g = qkv_input[0], out_cotangent[0]
    width = g.shape[1] // 2
    heads = width // HEAD
    chips = lax.axis_size("zh")
    core, chip, low = lax.axis_index("core"), lax.axis_index("zh"), lax.axis_index("zl")
    scalars = jnp.stack([core, chip]).astype(jnp.int32)
    fitting = (jnp.arange(8 * chips) // (4 * chips) == low // 2).astype(F32)[:, None]
    swap = [(0, 1), (1, 0)]
    line = ("zh", "core")

    def hops(by):
        later = [(2 * c, 2 * (c + by)) for c in range(chips - by)]
        return later + [(2 * (c + by) + 1, 2 * c + 1) for c in range(chips - by)]

    pairs = range(chips - 1)
    to_same = [(2 * c + 1, 2 * c + 3) for c in pairs] + [(2 * c + 2, 2 * c) for c in pairs]
    to_cross = [(2 * c + 1, 2 * c + 2) for c in pairs] + [(2 * c + 2, 2 * c + 1) for c in pairs]

    keep, send = call(
        pack_kernel, [((ROWS, 4 * width), BF16)] * 2, [pltpu.SemaphoreType.DMA((8,))],
        scalars, x, g, space=pl.BlockSpec(memory_space=pl.ANY), limit=8,
    )
    (taps,) = call(taps_kernel, [((TAPS, 4 * width), F32)], [], scalars, conv_weight, fitting)
    received = lax.ppermute(send, "core", swap)
    padded = [pltpu.VMEM((LONG, HEAD), F32)] * 4
    message, wrap = call(
        states_kernel,
        [((heads, HEAD + size, HEAD), BF16) for size in (2 * EDGE, EDGE)],
        padded + [pltpu.VMEM((PAIR, HEAD), BF16)] * 4,
        scalars, keep, received, taps,
    )
    same, cross = call(
        edge_rows_kernel, [((4, 3 * width), BF16)] * 2, [], scalars, keep, send, message
    )
    near = lax.ppermute(message, line, hops(1))
    far = lax.ppermute(message, line, hops(2))
    wrap = lax.ppermute(wrap, line, hops(3))
    same = lax.ppermute(same, line, to_same)
    cross = lax.ppermute(cross, line, to_cross)
    spread = lax.axis_size("yx")
    few = width // 2 // spread
    part = -(-TAPS * few // HEAD) * HEAD
    tail = ((16, width), BF16)
    products, fold, rows = call(
        products_kernel,
        [
            ((heads, TAPS, HEAD, HEAD), F32), ((width // 2, 2 * part), BF16),
            ((spread, width // 2), F32),
        ],
        padded, scalars, keep, received, taps, message,
    )
    inside, a, left_tail, b_tail, terms, front = call(
        inside_kernel,
        [
            ((EXT, width), F32), ((EXT, width), BF16), tail, tail, ((TAPS, width), F32),
            ((PRE + 8, width), F32),
        ],
        padded + [pltpu.VMEM((EXT, HEAD), BF16)] * 4,
        scalars, keep, received, same, cross, taps,
    )
    states, rows = call(
        terms_kernel, [((heads, HEAD, HEAD), BF16), ((spread, 1, 2 * part), F32)],
        [
            pltpu.VMEM((4, 16, width), F32), pltpu.VMEM((2, 16, width), BF16),
            pltpu.VMEM((TAPS, width), F32), pltpu.VMEM((2 * TAPS * spread, width // 2), F32),
        ],
        scalars, terms, products, a, front, left_tail, b_tail, near, far, wrap, taps, fold, rows,
    )
    rows = jnp.sum(lax.all_to_all(rows, "yx", 0, 0, tiled=True), (0, 1)).reshape(2, part)
    rows = jnp.broadcast_to(rows[None, None, :, None], (2, 2, 2, chips, part)).reshape(8 * chips, part)
    own, sent = call(
        input_kernel, [((ROWS, width), BF16)] * 2,
        [pltpu.VMEM((PAIR, width), BF16), pltpu.VMEM((EXT, width), F32)],
        scalars, inside, a, states, taps, rows,
    )
    rows = lax.all_to_all(rows, ("core", "zl", "zh"), 0, 0, tiled=True)
    share = jnp.sum(rows * fitting, 0)[: TAPS * few].reshape(TAPS, few)
    shares = share * (1.0 / (lax.axis_size("zl") * spread))
    other = lax.ppermute(sent, "core", swap)
    first, second = jnp.where(core == 0, own, other), jnp.where(core == 0, other, own)
    return jnp.concatenate([first, second], 1)[None], shares


def solution(mesh):
    dp, seq = mesh.shape["dp"], mesh.shape["seq"]
    fine = Mesh(mesh.devices.reshape(4, dp // 4, seq // 2, 2), ("zl", "yx", "zh", "core"))
    rows = P(("zl", "yx"), ("zh", "core"), None)
    return jax.shard_map(
        per_device, mesh=fine, in_specs=(rows, P(), rows),
        out_specs=(rows, P(None, ("zl", "yx"))), check_vma=False,
    )
```

```python
import jax
import jax.numpy as jnp
from jax import lax
from jax.experimental import pallas as pl
from jax.experimental.pallas import tpu as pltpu
from jax.sharding import Mesh
from jax.sharding import PartitionSpec as P

HEAD = 128
TAPS = 4
ROWS = 128
PAIR = 2 * ROWS
EXT = PAIR + 16
PRE = 8
LONG = PRE + PAIR + 8
EDGE = 8
F32 = jnp.float32
BF16 = jnp.bfloat16
LEFT, A, B, RAW = range(4)
VMEM = pl.BlockSpec(memory_space=pltpu.VMEM)
SMEM = pl.BlockSpec(memory_space=pltpu.SMEM)


def call(kernel, shapes, scratch, scalars, *arrays, space=VMEM, limit=16):
    return pl.pallas_call(
        kernel,
        out_shape=[jax.ShapeDtypeStruct(s, t) for s, t in shapes],
        in_specs=[SMEM] + [space] * len(arrays),
        out_specs=[VMEM] * len(shapes),
        scratch_shapes=scratch,
        compiler_params=pltpu.CompilerParams(vmem_limit_bytes=limit * 1024 * 1024),
    )(scalars, *arrays)


def nt(a, b):
    return lax.dot_general(a, b, (((1,), (1,)), ((), ())), preferred_element_type=F32)


def tn(a, b):
    return lax.dot_general(a, b, (((0,), (0,)), ((), ())), preferred_element_type=F32)


def nn(a, b):
    return lax.dot_general(a, b, (((1,), (0,)), ((), ())), preferred_element_type=F32)


def lanes(group, head, width):
    return slice(group * width + head * HEAD, group * width + (head + 1) * HEAD)


def fill_edges(core, keep_ref, send_ref, same_ref, cross_ref):
    width = keep_ref.shape[1] // 4
    edge = pl.ds(pl.multiple_of(core * (ROWS - 16), 16), 16)
    for ref, out_ref, later in ((keep_ref, same_ref, A), (send_ref, cross_ref, B)):
        for slot, (first, last) in enumerate(((LEFT, LEFT), (A, later), (B, RAW))):
            zero = ref[edge, first * width : (first + 1) * width].astype(F32)[0:4]
            one = ref[edge, last * width : (last + 1) * width].astype(F32)[12:16]
            rows = jnp.where(core == 1, one, zero).astype(BF16)
            out_ref[:, slot * width : (slot + 1) * width] = rows


def pack_kernel(scalars, x_ref, g_ref, keep_ref, send_ref, same_ref, cross_ref, sems):
    core = scalars[0]
    width = keep_ref.shape[1] // 4
    of_core = (
        ((x_ref, 3), (g_ref, 1), (x_ref, 5), (x_ref, 1)),
        ((x_ref, 0), (x_ref, 4), (g_ref, 0), (x_ref, 2)),
    )

    def fill(mine):
        copies = []

        def copy(source_ref, group, out_ref, slot):
            lanes_in = slice(group * width, (group + 1) * width)
            lanes_out = slice(slot * width, (slot + 1) * width)
            copies.append(
                pltpu.make_async_copy(
                    source_ref.at[:, lanes_in], out_ref.at[:, lanes_out], sems.at[len(copies)]
                )
            )

        for slot, (source_ref, group) in enumerate(of_core[1 - mine]):
            copy(source_ref, group, send_ref, slot)
        for slot, (source_ref, group) in enumerate(of_core[mine]):
            copy(source_ref, group, keep_ref, slot)
        for each in copies:
            each.start()
        for each in copies:
            each.wait()

    @pl.when(core == 0)
    def _():
        fill(0)

    @pl.when(core == 1)
    def _():
        fill(1)

    fill_edges(core, keep_ref, send_ref, same_ref, cross_ref)


def taps_kernel(scalars, w_ref, fitting_ref, taps_ref):
    width = taps_ref.shape[1] // 4
    row = lax.broadcasted_iota(jnp.int32, (TAPS, width), 0)
    unit = jnp.where(row == 0, 1.0, 0.0).astype(F32)
    for core, groups in enumerate(((3, None, 5, 1), (0, 4, None, 2))):

        @pl.when(scalars[0] == core)
        def _():
            for slot, group in enumerate(groups):
                part = unit if group is None else w_ref[:, group * width : (group + 1) * width]
                taps_ref[:, slot * width : (slot + 1) * width] = part


def gather_rows(core, keep_ref, received_ref, at, padded_ref):
    own = pl.ds(pl.multiple_of(PRE + core * ROWS, 8), ROWS)
    other = pl.ds(pl.multiple_of(PRE + (1 - core) * ROWS, 8), ROWS)
    padded_ref[own, :] = keep_ref[:, at].astype(F32)
    padded_ref[other, :] = received_ref[:, at].astype(F32)


def convolved(padded_ref, taps, start, count):
    total = taps[0:1] * padded_ref[start : start + count, :]
    for j in range(1, TAPS):
        total = total + taps[j : j + 1] * padded_ref[start - j : start - j + count, :]
    return total


def states_kernel(scalars, keep_ref, received_ref, taps_ref, message_ref, wrap_ref, *scratch):
    core, chip = scalars[0], scalars[1]
    width = keep_ref.shape[1] // 4
    padded_refs, value_refs = scratch[:4], scratch[4:]
    for ref in padded_refs:
        ref[0:PRE, :] = jnp.zeros((PRE, HEAD), F32)
    row = lax.broadcasted_iota(jnp.int32, (ROWS, HEAD), 0)
    kept_rows = (row >= TAPS - 1) | (chip == 0)
    first_rows = jnp.where(chip == 0, 0.0, 1.0)
    for head in range(width // HEAD):
        firsts, lasts = [], []
        for turn, group in enumerate((LEFT, B)):
            padded_ref = padded_refs[(2 * head + turn) % 4]
            value_ref = value_refs[(2 * head + turn) % 4]
            at = lanes(group, head, width)
            gather_rows(core, keep_ref, received_ref, at, padded_ref)
            taps = taps_ref[:, at]
            for first in (0, ROWS):
                total = convolved(padded_ref, taps, PRE + first, ROWS)
                if group == LEFT and first == 0:
                    total = jnp.where(kept_rows, total, 0.0)
                value_ref[first : first + ROWS, :] = total.astype(BF16)
            front = padded_ref[PRE : PRE + 4, :]
            firsts.append(front * first_rows if group == LEFT else front)
            lasts.append(padded_ref[PRE + PAIR - 4 : PRE + PAIR, :])
        left, right = value_refs[(2 * head) % 4], value_refs[(2 * head + 1) % 4]
        state = tn(right[...], left[...]).astype(BF16)
        firsts, lasts = jnp.concatenate(firsts, 0), jnp.concatenate(lasts, 0)
        for ref in (message_ref, wrap_ref):
            ref[head, 0:HEAD, :] = state
        message_ref[head, HEAD:, :] = jnp.concatenate([firsts, lasts], 0).astype(BF16)
        wrap_ref[head, HEAD:, :] = jnp.where(core == 0, lasts, firsts).astype(BF16)


def hold_kernel(scalars, same_ref, cross_ref, after_ref, same_out_ref, cross_out_ref):
    same_out_ref[...] = same_ref[...]
    cross_out_ref[...] = cross_ref[...]


def products_kernel(
    scalars, keep_ref, received_ref, taps_ref, after_ref, products_ref, fold_ref, rows_ref, *padded_refs
):
    core = scalars[0]
    width = keep_ref.shape[1] // 4
    for ref in padded_refs:
        ref[0:PRE, :] = jnp.zeros((PRE, HEAD), F32)
    row = lax.broadcasted_iota(jnp.int32, (PAIR, HEAD), 0)
    for head in range(width // HEAD):
        a_ref, raw_ref = (padded_refs[(2 * head + k) % 4] for k in range(2))
        at = lanes(A, head, width)
        gather_rows(core, keep_ref, received_ref, at, a_ref)
        gather_rows(core, keep_ref, received_ref, lanes(RAW, head, width), raw_ref)
        a = convolved(a_ref, taps_ref[:, at], PRE, PAIR)
        a = jnp.where(row >= TAPS - 1, a, 0.0).astype(BF16)
        for j in range(TAPS):
            shifted = raw_ref[PRE - j : PRE - j + PAIR, :].astype(BF16)
            products_ref[head, j] = tn(a, shifted) * (1.0 / HEAD)
    few = width // 2 // rows_ref.shape[0]
    place = lax.broadcasted_iota(jnp.int32, fold_ref.shape, 1)
    column = lax.broadcasted_iota(jnp.int32, fold_ref.shape, 0)
    place = lax.rem(place, fold_ref.shape[1] // 2)
    fits = (lax.rem(column, few) == lax.rem(place, few)) & (place < TAPS * few)
    fold_ref[...] = jnp.where(fits, 1.0, 0.0).astype(BF16)
    device = lax.broadcasted_iota(jnp.int32, rows_ref.shape, 0) * few
    column = lax.broadcasted_iota(jnp.int32, rows_ref.shape, 1)
    rows_ref[...] = jnp.where((column >= device) & (column < device + few), 1.0, 0.0)


def inside_kernel(
    scalars, keep_ref, received_ref, same_ref, cross_ref, taps_ref,
    kept_ref, a_ref, left_tail_ref, b_tail_ref, terms_ref, front_ref, *scratch,
):
    core = scalars[0]
    width = keep_ref.shape[1] // 4
    padded_refs, value_refs = scratch[:4], scratch[4:]
    same, cross = same_ref[...].astype(F32), cross_ref[...].astype(F32)
    before, after = jnp.where(core == 1, same, cross), jnp.where(core == 1, cross, same)
    row = lax.broadcasted_iota(jnp.int32, (EXT, EXT), 0)
    column = lax.broadcasted_iota(jnp.int32, (EXT, EXT), 1)
    causal = jnp.where(column <= row, 1.0 / HEAD, 0.0)
    reverse = jnp.where(
        (column >= row) & (column < PAIR),
        1.0 / HEAD,
        jnp.where((column >= PAIR) & (column < row), -1.0 / HEAD, 0.0),
    )
    mask = jnp.where(core == 0, causal, reverse)
    none = jnp.zeros((4, HEAD), F32)
    tail_row = lax.broadcasted_iota(jnp.int32, (16, HEAD), 0)
    tail_used = (tail_row < TAPS - 1) & (core == 1)
    turn = 0
    for head in range(width // HEAD):
        to = lanes(0, head, width)
        values = []
        for group in (LEFT, A, B, RAW):
            padded_ref = padded_refs[turn % 4]
            value_ref = value_refs[turn % 4]
            turn += 1
            at = lanes(group, head, width)
            gather_rows(core, keep_ref, received_ref, at, padded_ref)
            front = before[:, lanes((0, 1, 1, 2)[group], head, width)]
            back = after[:, lanes((0, 1, 2, 2)[group], head, width)]
            padded_ref[0:PRE, :] = jnp.concatenate([none, front], 0)
            padded_ref[PRE + PAIR : LONG, :] = jnp.concatenate([back, none], 0)
            if group == RAW:
                raw_ref = padded_ref
                continue
            taps = taps_ref[:, at]
            for first in (0, ROWS):
                total = convolved(padded_ref, taps, PRE + first, ROWS)
                value_ref[first : first + ROWS, :] = total.astype(BF16)
            tail = convolved(padded_ref, taps, PRE + PAIR, 8)
            tail = jnp.concatenate([tail, jnp.zeros((8, HEAD), F32)], 0)
            value_ref[PAIR:EXT, :] = tail.astype(BF16)
            if group != A:
                tail_ref = left_tail_ref if group == LEFT else b_tail_ref
                tail_ref[:, to] = jnp.where(tail_used, tail, 0.0).astype(BF16)
            values.append(value_ref)
        left, a, b = (ref[...] for ref in values)
        a_ref[:, to] = a
        scores = (nt(a, b) * mask).astype(BF16)
        kept_ref[:, to] = nn(scores, left)
        front_ref[:, to] = raw_ref[0 : PRE + 8, :]
        sums = [jnp.zeros((8, HEAD), F32)] * TAPS
        for first in range(0, PAIR, 64):
            kept = kept_ref[first : first + 64, to]
            for j in range(TAPS):
                start = PRE + first - j
                term = kept * raw_ref[start : start + 64, :]
                sums[j] = sums[j] + jnp.sum(term.reshape(8, 8, HEAD), 0)
        terms_ref[:, to] = jnp.concatenate([jnp.sum(s, 0, keepdims=True) for s in sums], 0)


def terms_kernel(
    scalars, terms_ref, products_ref, a_ref, front_ref, left_tail_ref, b_tail_ref,
    near_ref, far_ref, wrap_ref, taps_ref, fold_ref, rows_ref,
    states_ref, shares_ref, edge_ref, seam_ref, total_ref, stack_ref,
):
    core = scalars[0]
    heads, width = products_ref.shape[0], terms_ref.shape[1]
    none = jnp.zeros((8, HEAD), F32)
    for head in range(heads):
        to = lanes(0, head, width)
        near, far, wrap = (r[head, HEAD:, :].astype(F32) for r in (near_ref, far_ref, wrap_ref))
        near = jnp.where(core == 0, near[0:EDGE], near[EDGE : 2 * EDGE])
        first, last = far[0:EDGE], far[EDGE : 2 * EDGE]
        for turn, (zero, one) in enumerate((((last, near), (near, first)), ((wrap, first), (last, wrap)))):
            before, after = (jnp.where(core == 0, *pair) for pair in zip(zero, one))
            for slot, at in enumerate((slice(0, 4), slice(4, 8))):
                edge_ref[2 * slot + turn, 0:8, to] = jnp.concatenate([before[at], after[at]], 0)
                edge_ref[2 * slot + turn, 8:16, to] = none
    row = lax.broadcasted_iota(jnp.int32, (8, width), 0)
    for slot, group, tail_ref in ((0, LEFT, left_tail_ref), (1, B, b_tail_ref)):
        taps = taps_ref[:, group * width : (group + 1) * width]
        rows = [convolved(edge_ref.at[2 * slot + turn], taps, 4, 8) for turn in range(2)]
        rows = [jnp.where(row < TAPS - 1, total, 0.0) for total in rows]
        seam_ref[slot, 0:16, :] = jnp.concatenate(rows, 0).astype(BF16)
        seam_ref[slot, 16:32, :] = tail_ref[...]
    every = [(head, lanes(0, head, width)) for head in range(heads)]
    seams = [tn(seam_ref[1, :, to], seam_ref[0, :, to]) for _, to in every]
    states = []
    for (head, _), seam in zip(every, seams):
        near, far, wrap = (r[head, 0:HEAD, :].astype(F32) for r in (near_ref, far_ref, wrap_ref))
        states.append((near + far + (wrap + seam)).astype(BF16))
    fronts = [nn(a_ref[0:16, to], state) for (_, to), state in zip(every, states)]
    row = lax.broadcasted_iota(jnp.int32, (8, HEAD), 0)
    for (head, to), state, front in zip(every, states, fronts):
        states_ref[head] = state
        state = state.astype(F32)
        front = jnp.where(row < TAPS - 1, front[0:8] * (1.0 / HEAD), 0.0)
        sums = []
        for j in range(TAPS):
            product = (state * products_ref[head, j]).reshape(HEAD // 8, 8, HEAD)
            total = jnp.sum(product, 0) + front * front_ref[PRE - j : PRE - j + 8, to]
            sums.append(jnp.sum(total, 0, keepdims=True))
        total_ref[:, to] = terms_ref[:, to] + jnp.concatenate(sums, 0)
    half = width // 2
    spread = rows_ref.shape[0]
    fitting = rows_ref[...]
    for part in range(2):
        for j in range(TAPS):
            at = (part * TAPS + j) * spread
            line = total_ref[j : j + 1, part * half : (part + 1) * half]
            stack_ref[at : at + spread, :] = fitting * line
    folded = nn(stack_ref[...].astype(BF16), fold_ref[...])
    few = half // spread
    place = lax.broadcasted_iota(jnp.int32, (spread, fold_ref.shape[1]), 1)
    gathered = jnp.zeros((spread, fold_ref.shape[1]), F32)
    for part in range(2):
        for j in range(TAPS):
            at = (part * TAPS + j) * spread
            begin = part * (fold_ref.shape[1] // 2) + j * few
            here = (place >= begin) & (place < begin + few)
            gathered = gathered + jnp.where(here, folded[at : at + spread], 0.0)
    shares_ref[...] = gathered.reshape(shares_ref.shape)


def input_kernel(
    scalars, inside_ref, a_ref, states_ref, taps_ref, after_ref, own_ref, send_ref, grad_ref, kept_ref
):
    core = scalars[0]
    width = own_ref.shape[1]
    for head in range(width // HEAD):
        to = lanes(0, head, width)
        kept_ref[:, to] = inside_ref[:, to] + nn(a_ref[:, to], states_ref[head]) * (1.0 / HEAD)
        taps = taps_ref[:, lanes(RAW, head, width)]
        for first in range(0, PAIR, 64):
            grad = taps[0:1] * kept_ref[first : first + 64, to]
            for j in range(1, TAPS):
                grad = grad + taps[j : j + 1] * kept_ref[first + j : first + j + 64, to]
            grad_ref[first : first + 64, to] = grad.astype(BF16)
    own_ref[...] = grad_ref[pl.ds(pl.multiple_of(core * ROWS, ROWS), ROWS), :]
    send_ref[...] = grad_ref[pl.ds(pl.multiple_of((1 - core) * ROWS, ROWS), ROWS), :]


def join_kernel(scalars, own_ref, other_ref, out_ref):
    width = own_ref.shape[1]
    for core, parts in enumerate(((own_ref, other_ref), (other_ref, own_ref))):

        @pl.when(scalars[0] == core)
        def _():
            for half, part in enumerate(parts):
                out_ref[:, half * width : (half + 1) * width] = part[...]


def per_device(qkv_input, conv_weight, out_cotangent):
    x, g = qkv_input[0], out_cotangent[0]
    width = g.shape[1] // 2
    heads = width // HEAD
    chips = lax.axis_size("zh")
    core, chip, low = lax.axis_index("core"), lax.axis_index("zh"), lax.axis_index("zl")
    scalars = jnp.stack([core, chip]).astype(jnp.int32)
    fitting = (jnp.arange(8 * chips) // (4 * chips) == low // 2).astype(F32)[:, None]
    swap = [(0, 1), (1, 0)]
    line = ("zh", "core")

    def hops(by):
        later = [(2 * c, 2 * (c + by)) for c in range(chips - by)]
        return later + [(2 * (c + by) + 1, 2 * c + 1) for c in range(chips - by)]

    pairs = range(chips - 1)
    to_same = [(2 * c + 1, 2 * c + 3) for c in pairs] + [(2 * c + 2, 2 * c) for c in pairs]
    to_cross = [(2 * c + 1, 2 * c + 2) for c in pairs] + [(2 * c + 2, 2 * c + 1) for c in pairs]

    keep, send, same, cross = call(
        pack_kernel, [((ROWS, 4 * width), BF16)] * 2 + [((4, 3 * width), BF16)] * 2,
        [pltpu.SemaphoreType.DMA((8,))],
        scalars, x, g, space=pl.BlockSpec(memory_space=pl.ANY), limit=8,
    )
    (taps,) = call(taps_kernel, [((TAPS, 4 * width), F32)], [], scalars, conv_weight, fitting)
    received = lax.ppermute(send, "core", swap)
    padded = [pltpu.VMEM((LONG, HEAD), F32)] * 4
    message, wrap = call(
        states_kernel,
        [((heads, HEAD + size, HEAD), BF16) for size in (2 * EDGE, EDGE)],
        padded + [pltpu.VMEM((PAIR, HEAD), BF16)] * 4,
        scalars, keep, received, taps,
    )
    same, cross = call(
        hold_kernel, [((4, 3 * width), BF16)] * 2, [], scalars, same, cross, message
    )
    near = lax.ppermute(message, line, hops(1))
    far = lax.ppermute(message, line, hops(2))
    wrap = lax.ppermute(wrap, line, hops(3))
    same = lax.ppermute(same, line, to_same)
    cross = lax.ppermute(cross, line, to_cross)
    spread = lax.axis_size("yx")
    few = width // 2 // spread
    part = -(-TAPS * few // HEAD) * HEAD
    tail = ((16, width), BF16)
    products, fold, rows = call(
        products_kernel,
        [
            ((heads, TAPS, HEAD, HEAD), F32), ((width // 2, 2 * part), BF16),
            ((spread, width // 2), F32),
        ],
        padded, scalars, keep, received, taps, message,
    )
    inside, a, left_tail, b_tail, terms, front = call(
        inside_kernel,
        [
            ((EXT, width), F32), ((EXT, width), BF16), tail, tail, ((TAPS, width), F32),
            ((PRE + 8, width), F32),
        ],
        padded + [pltpu.VMEM((EXT, HEAD), BF16)] * 4,
        scalars, keep, received, same, cross, taps,
    )
    states, rows = call(
        terms_kernel, [((heads, HEAD, HEAD), BF16), ((spread, 1, 2 * part), F32)],
        [
            pltpu.VMEM((4, 16, width), F32), pltpu.VMEM((2, 32, width), BF16),
            pltpu.VMEM((TAPS, width), F32), pltpu.VMEM((2 * TAPS * spread, width // 2), F32),
        ],
        scalars, terms, products, a, front, left_tail, b_tail, near, far, wrap, taps, fold, rows,
    )
    rows = jnp.sum(lax.all_to_all(rows, "yx", 0, 0, tiled=True), (0, 1)).reshape(2, part)
    rows = jnp.broadcast_to(rows[None, None, :, None], (2, 2, 2, chips, part)).reshape(8 * chips, part)
    own, sent = call(
        input_kernel, [((ROWS, width), BF16)] * 2,
        [pltpu.VMEM((PAIR, width), BF16), pltpu.VMEM((EXT, width), F32)],
        scalars, inside, a, states, taps, rows,
    )
    rows = lax.all_to_all(rows, ("core", "zl", "zh"), 0, 0, tiled=True)
    share = jnp.sum(rows * fitting, 0)[: TAPS * few].reshape(TAPS, few)
    shares = share * (1.0 / (lax.axis_size("zl") * spread))
    other = lax.ppermute(sent, "core", swap)
    (grad,) = call(join_kernel, [((ROWS, 2 * width), BF16)], [], scalars, own, other)
    return grad[None], shares


def solution(mesh):
    dp, seq = mesh.shape["dp"], mesh.shape["seq"]
    fine = Mesh(mesh.devices.reshape(4, dp // 4, seq // 2, 2), ("zl", "yx", "zh", "core"))
    rows = P(("zl", "yx"), ("zh", "core"), None)
    return jax.shard_map(
        per_device, mesh=fine, in_specs=(rows, P(), rows),
        out_specs=(rows, P(None, ("zl", "yx"))), check_vma=False,
    )
```

```python
import jax
import jax.numpy as jnp
from jax import lax
from jax.experimental import pallas as pl
from jax.experimental.pallas import tpu as pltpu
from jax.sharding import Mesh
from jax.sharding import PartitionSpec as P

HEAD = 128
TAPS = 4
ROWS = 128
PAIR = 2 * ROWS
EXT = PAIR + 16
PRE = 8
LONG = PRE + PAIR + 8
EDGE = 8
F32 = jnp.float32
BF16 = jnp.bfloat16
LEFT, A, B, RAW = range(4)
VMEM = pl.BlockSpec(memory_space=pltpu.VMEM)
SMEM = pl.BlockSpec(memory_space=pltpu.SMEM)


def call(kernel, shapes, scratch, scalars, *arrays, space=VMEM, limit=16):
    return pl.pallas_call(
        kernel,
        out_shape=[jax.ShapeDtypeStruct(s, t) for s, t in shapes],
        in_specs=[SMEM] + [space] * len(arrays),
        out_specs=[VMEM] * len(shapes),
        scratch_shapes=scratch,
        compiler_params=pltpu.CompilerParams(vmem_limit_bytes=limit * 1024 * 1024),
    )(scalars, *arrays)


def nt(a, b):
    return lax.dot_general(a, b, (((1,), (1,)), ((), ())), preferred_element_type=F32)


def tn(a, b):
    return lax.dot_general(a, b, (((0,), (0,)), ((), ())), preferred_element_type=F32)


def nn(a, b):
    return lax.dot_general(a, b, (((1,), (0,)), ((), ())), preferred_element_type=F32)


def lanes(group, head, width):
    return slice(group * width + head * HEAD, group * width + (head + 1) * HEAD)


def fill_edges(core, keep_ref, send_ref):
    width = keep_ref.shape[1] // 4
    edge = pl.ds(pl.multiple_of(core * (ROWS - 16), 16), 16)
    none = jnp.zeros((12, width), F32)
    for slot, (first, last) in enumerate(((LEFT, LEFT), (A, A), (B, RAW), (RAW, RAW))):
        zero = keep_ref[edge, first * width : (first + 1) * width].astype(F32)[0:4]
        one = keep_ref[edge, last * width : (last + 1) * width].astype(F32)[12:16]
        rows = jnp.concatenate([jnp.where(core == 1, one, zero), none], 0)
        send_ref[ROWS : ROWS + 16, slot * width : (slot + 1) * width] = rows.astype(BF16)


def pack_kernel(scalars, x_ref, g_ref, before_ref, keep_ref, send_ref, sems):
    core = scalars[0]
    width = keep_ref.shape[1] // 4
    of_core = (
        ((x_ref, 3), (g_ref, 1), (x_ref, 5), (x_ref, 1)),
        ((x_ref, 0), (x_ref, 4), (g_ref, 0), (x_ref, 2)),
    )

    def fill(mine):
        copies = []

        def copy(source_ref, group, out_ref, slot):
            lanes_in = slice(group * width, (group + 1) * width)
            lanes_out = slice(slot * width, (slot + 1) * width)
            copies.append(
                pltpu.make_async_copy(
                    source_ref.at[:, lanes_in], out_ref.at[0:ROWS, lanes_out], sems.at[len(copies)]
                )
            )

        for slot, (source_ref, group) in enumerate(of_core[1 - mine]):
            copy(source_ref, group, send_ref, slot)
        for slot, (source_ref, group) in enumerate(of_core[mine]):
            copy(source_ref, group, keep_ref, slot)
        for each in copies:
            each.start()
        for each in copies:
            each.wait()

    @pl.when(core == 0)
    def _():
        fill(0)

    @pl.when(core == 1)
    def _():
        fill(1)

    fill_edges(core, keep_ref, send_ref)


def taps_kernel(scalars, w_ref, taps_ref):
    width = taps_ref.shape[1] // 4
    row = lax.broadcasted_iota(jnp.int32, (TAPS, width), 0)
    unit = jnp.where(row == 0, 1.0, 0.0).astype(F32)
    for core, groups in enumerate(((3, None, 5, 1), (0, 4, None, 2))):

        @pl.when(scalars[0] == core)
        def _():
            for slot, group in enumerate(groups):
                part = unit if group is None else w_ref[:, group * width : (group + 1) * width]
                taps_ref[:, slot * width : (slot + 1) * width] = part


def gather_rows(core, keep_ref, received_ref, at, padded_ref):
    own = pl.ds(pl.multiple_of(PRE + core * ROWS, 8), ROWS)
    other = pl.ds(pl.multiple_of(PRE + (1 - core) * ROWS, 8), ROWS)
    padded_ref[own, :] = keep_ref[:, at].astype(F32)
    padded_ref[other, :] = received_ref[0:ROWS, at].astype(F32)


def convolved(padded_ref, taps, start, count):
    total = taps[0:1] * padded_ref[start : start + count, :]
    for j in range(1, TAPS):
        total = total + taps[j : j + 1] * padded_ref[start - j : start - j + count, :]
    return total


def half_of(one_ref, two_ref, head):
    first = one_ref.shape[0]
    return (one_ref, head) if head < first else (two_ref, head - first)


def states_kernel(scalars, keep_ref, received_ref, taps_ref, one_ref, two_ref, wrap_ref, *scratch):
    core, chip = scalars[0], scalars[1]
    width = keep_ref.shape[1] // 4
    padded_refs, value_refs = scratch[:4], scratch[4:]
    for ref in padded_refs:
        ref[0:PRE, :] = jnp.zeros((PRE, HEAD), F32)
    row = lax.broadcasted_iota(jnp.int32, (ROWS, HEAD), 0)
    kept_rows = (row >= TAPS - 1) | (chip == 0)
    first_rows = jnp.where(chip == 0, 0.0, 1.0)
    for head in range(width // HEAD):
        firsts, lasts = [], []
        for turn, group in enumerate((LEFT, B)):
            padded_ref = padded_refs[(2 * head + turn) % 4]
            value_ref = value_refs[(2 * head + turn) % 4]
            at = lanes(group, head, width)
            gather_rows(core, keep_ref, received_ref, at, padded_ref)
            taps = taps_ref[:, at]
            for first in (0, ROWS):
                total = convolved(padded_ref, taps, PRE + first, ROWS)
                if group == LEFT and first == 0:
                    total = jnp.where(kept_rows, total, 0.0)
                value_ref[first : first + ROWS, :] = total.astype(BF16)
            front = padded_ref[PRE : PRE + 4, :]
            firsts.append(front * first_rows if group == LEFT else front)
            lasts.append(padded_ref[PRE + PAIR - 4 : PRE + PAIR, :])
        left, right = value_refs[(2 * head) % 4], value_refs[(2 * head + 1) % 4]
        state = tn(right[...], left[...]).astype(BF16)
        firsts, lasts = jnp.concatenate(firsts, 0), jnp.concatenate(lasts, 0)
        message_ref, at = half_of(one_ref, two_ref, head)
        message_ref[at, 0:HEAD, :] = state
        third = jnp.where(
            core == 0,
            received_ref[ROWS - 16 : ROWS, lanes(RAW, head, width)].astype(F32)[12:16],
            received_ref[0:16, lanes(A, head, width)].astype(F32)[0:4],
        )
        others = [
            received_ref[ROWS : ROWS + 16, lanes(slot, head, width)].astype(F32)[0:4] for slot in range(3)
        ]
        message_ref[at, HEAD:, :] = jnp.concatenate([firsts, lasts, third, *others], 0).astype(BF16)
        wrap_ref[head, 0:HEAD, :] = state
        wrap_ref[head, HEAD:, :] = jnp.where(core == 0, lasts, firsts).astype(BF16)


def partner_kernel(scalars, near_one_ref, near_two_ref, out_ref):
    width = out_ref.shape[1] // 3
    for head in range(width // HEAD):
        near_ref, at = half_of(near_one_ref, near_two_ref, head)
        rows = near_ref[at, HEAD + 2 * EDGE :, :].astype(F32)
        for slot in range(3):
            out_ref[:, lanes(slot, head, width)] = rows[4 * slot + 4 : 4 * slot + 8].astype(BF16)


def hand_on_kernel(scalars, message_ref, after_ref, out_ref):
    out_ref[...] = message_ref[:, 0 : out_ref.shape[1], :]


def products_kernel(
    scalars, keep_ref, received_ref, taps_ref, after_ref, products_ref, fold_ref, rows_ref, *padded_refs
):
    core = scalars[0]
    width = keep_ref.shape[1] // 4
    for ref in padded_refs:
        ref[0:PRE, :] = jnp.zeros((PRE, HEAD), F32)
    row = lax.broadcasted_iota(jnp.int32, (PAIR, HEAD), 0)
    for head in range(width // HEAD):
        a_ref, raw_ref = (padded_refs[(2 * head + k) % 4] for k in range(2))
        at = lanes(A, head, width)
        gather_rows(core, keep_ref, received_ref, at, a_ref)
        gather_rows(core, keep_ref, received_ref, lanes(RAW, head, width), raw_ref)
        a = convolved(a_ref, taps_ref[:, at], PRE, PAIR)
        a = jnp.where(row >= TAPS - 1, a, 0.0).astype(BF16)
        for j in range(TAPS):
            shifted = raw_ref[PRE - j : PRE - j + PAIR, :].astype(BF16)
            products_ref[head, j] = tn(a, shifted) * (1.0 / HEAD)
    few = width // 2 // rows_ref.shape[0]
    place = lax.broadcasted_iota(jnp.int32, fold_ref.shape, 1)
    column = lax.broadcasted_iota(jnp.int32, fold_ref.shape, 0)
    place = lax.rem(place, fold_ref.shape[1] // 2)
    fits = (lax.rem(column, few) == lax.rem(place, few)) & (place < TAPS * few)
    fold_ref[...] = jnp.where(fits, 1.0, 0.0).astype(BF16)
    device = lax.broadcasted_iota(jnp.int32, rows_ref.shape, 0) * few
    column = lax.broadcasted_iota(jnp.int32, rows_ref.shape, 1)
    rows_ref[...] = jnp.where((column >= device) & (column < device + few), 1.0, 0.0)


def inside_kernel(
    scalars, keep_ref, received_ref, near_one_ref, near_two_ref, other_ref, taps_ref,
    kept_ref, a_ref, left_tail_ref, b_tail_ref, terms_ref, front_ref, *scratch,
):
    core = scalars[0]
    width = keep_ref.shape[1] // 4
    padded_refs, value_refs = scratch[:4], scratch[4:]
    other = other_ref[...].astype(F32)
    row = lax.broadcasted_iota(jnp.int32, (EXT, EXT), 0)
    column = lax.broadcasted_iota(jnp.int32, (EXT, EXT), 1)
    causal = jnp.where(column <= row, 1.0 / HEAD, 0.0)
    reverse = jnp.where(
        (column >= row) & (column < PAIR),
        1.0 / HEAD,
        jnp.where((column >= PAIR) & (column < row), -1.0 / HEAD, 0.0),
    )
    mask = jnp.where(core == 0, causal, reverse)
    none = jnp.zeros((4, HEAD), F32)
    tail_row = lax.broadcasted_iota(jnp.int32, (16, HEAD), 0)
    tail_used = (tail_row < TAPS - 1) & (core == 1)
    turn = 0
    for head in range(width // HEAD):
        to = lanes(0, head, width)
        values = []
        near_ref, half = half_of(near_one_ref, near_two_ref, head)
        near = near_ref[half, HEAD:, :].astype(F32)
        first, last, third = near[0:EDGE], near[EDGE : 2 * EDGE], near[2 * EDGE : 2 * EDGE + 4]
        partner = [other[:, lanes(slot, head, width)] for slot in range(3)]
        befores = zip((last[0:4], third, last[4:8], third), (partner[0], partner[1], partner[1], partner[2]))
        afters = zip((partner[0], partner[1], partner[2], third), (first[0:4], third, first[4:8], third))
        befores, afters = ([jnp.where(core == 0, *pair) for pair in pairs] for pairs in (befores, afters))
        for group in (LEFT, A, B, RAW):
            padded_ref = padded_refs[turn % 4]
            value_ref = value_refs[turn % 4]
            turn += 1
            at = lanes(group, head, width)
            gather_rows(core, keep_ref, received_ref, at, padded_ref)
            padded_ref[0:PRE, :] = jnp.concatenate([none, befores[group]], 0)
            padded_ref[PRE + PAIR : LONG, :] = jnp.concatenate([afters[group], none], 0)
            if group == RAW:
                raw_ref = padded_ref
                continue
            taps = taps_ref[:, at]
            for first in (0, ROWS):
                total = convolved(padded_ref, taps, PRE + first, ROWS)
                value_ref[first : first + ROWS, :] = total.astype(BF16)
            tail = convolved(padded_ref, taps, PRE + PAIR, 8)
            tail = jnp.concatenate([tail, jnp.zeros((8, HEAD), F32)], 0)
            value_ref[PAIR:EXT, :] = tail.astype(BF16)
            if group != A:
                tail_ref = left_tail_ref if group == LEFT else b_tail_ref
                tail_ref[:, to] = jnp.where(tail_used, tail, 0.0).astype(BF16)
            values.append(value_ref)
        left, a, b = (ref[...] for ref in values)
        a_ref[:, to] = a
        scores = (nt(a, b) * mask).astype(BF16)
        kept_ref[:, to] = nn(scores, left)
        front_ref[:, to] = raw_ref[0 : PRE + 8, :]
        sums = [jnp.zeros((8, HEAD), F32)] * TAPS
        for first in range(0, PAIR, 64):
            kept = kept_ref[first : first + 64, to]
            for j in range(TAPS):
                start = PRE + first - j
                term = kept * raw_ref[start : start + 64, :]
                sums[j] = sums[j] + jnp.sum(term.reshape(8, 8, HEAD), 0)
        terms_ref[:, to] = jnp.concatenate([jnp.sum(s, 0, keepdims=True) for s in sums], 0)


def terms_kernel(
    scalars, terms_ref, products_ref, a_ref, front_ref, left_tail_ref, b_tail_ref,
    near_one_ref, near_two_ref, far_one_ref, far_two_ref, wrap_ref, taps_ref, fold_ref, rows_ref,
    states_ref, shares_ref, edge_ref, seam_ref, total_ref, stack_ref,
):
    core = scalars[0]
    heads, width = products_ref.shape[0], terms_ref.shape[1]
    none = jnp.zeros((8, HEAD), F32)
    for head in range(heads):
        to = lanes(0, head, width)
        near_ref, at = half_of(near_one_ref, near_two_ref, head)
        far_ref, _ = half_of(far_one_ref, far_two_ref, head)
        near, far = (r[at, HEAD : HEAD + 2 * EDGE, :].astype(F32) for r in (near_ref, far_ref))
        wrap = wrap_ref[head, HEAD:, :].astype(F32)
        near = jnp.where(core == 0, near[0:EDGE], near[EDGE : 2 * EDGE])
        first, last = far[0:EDGE], far[EDGE : 2 * EDGE]
        for turn, (zero, one) in enumerate((((last, near), (near, first)), ((wrap, first), (last, wrap)))):
            before, after = (jnp.where(core == 0, *pair) for pair in zip(zero, one))
            for slot, at in enumerate((slice(0, 4), slice(4, 8))):
                edge_ref[2 * slot + turn, 0:8, to] = jnp.concatenate([before[at], after[at]], 0)
                edge_ref[2 * slot + turn, 8:16, to] = none
    row = lax.broadcasted_iota(jnp.int32, (8, width), 0)
    for slot, group, tail_ref in ((0, LEFT, left_tail_ref), (1, B, b_tail_ref)):
        taps = taps_ref[:, group * width : (group + 1) * width]
        rows = [convolved(edge_ref.at[2 * slot + turn], taps, 4, 8) for turn in range(2)]
        rows = [jnp.where(row < TAPS - 1, total, 0.0) for total in rows]
        seam_ref[slot, 0:16, :] = jnp.concatenate(rows, 0).astype(BF16)
        seam_ref[slot, 16:32, :] = tail_ref[...]
    every = [(head, lanes(0, head, width)) for head in range(heads)]
    seams = [tn(seam_ref[1, :, to], seam_ref[0, :, to]) for _, to in every]
    states = []
    for (head, _), seam in zip(every, seams):
        near_ref, at = half_of(near_one_ref, near_two_ref, head)
        far_ref, _ = half_of(far_one_ref, far_two_ref, head)
        near, far = (r[at, 0:HEAD, :].astype(F32) for r in (near_ref, far_ref))
        wrap = wrap_ref[head, 0:HEAD, :].astype(F32)
        states.append((near + far + (wrap + seam)).astype(BF16))
    fronts = [nn(a_ref[0:16, to], state) for (_, to), state in zip(every, states)]
    row = lax.broadcasted_iota(jnp.int32, (8, HEAD), 0)
    for (head, to), state, front in zip(every, states, fronts):
        states_ref[head] = state
        state = state.astype(F32)
        front = jnp.where(row < TAPS - 1, front[0:8] * (1.0 / HEAD), 0.0)
        sums = []
        for j in range(TAPS):
            product = (state * products_ref[head, j]).reshape(HEAD // 8, 8, HEAD)
            total = jnp.sum(product, 0) + front * front_ref[PRE - j : PRE - j + 8, to]
            sums.append(jnp.sum(total, 0, keepdims=True))
        total_ref[:, to] = terms_ref[:, to] + jnp.concatenate(sums, 0)
    half = width // 2
    spread = rows_ref.shape[0]
    fitting = rows_ref[...]
    for part in range(2):
        for j in range(TAPS):
            at = (part * TAPS + j) * spread
            line = total_ref[j : j + 1, part * half : (part + 1) * half]
            stack_ref[at : at + spread, :] = fitting * line
    folded = nn(stack_ref[...].astype(BF16), fold_ref[...])
    few = half // spread
    place = lax.broadcasted_iota(jnp.int32, (spread, fold_ref.shape[1]), 1)
    gathered = jnp.zeros((spread, fold_ref.shape[1]), F32)
    for part in range(2):
        for j in range(TAPS):
            at = (part * TAPS + j) * spread
            begin = part * (fold_ref.shape[1] // 2) + j * few
            here = (place >= begin) & (place < begin + few)
            gathered = gathered + jnp.where(here, folded[at : at + spread], 0.0)
    shares_ref[...] = gathered.reshape(shares_ref.shape)


def input_kernel(
    scalars, inside_ref, a_ref, states_ref, taps_ref, after_ref, own_ref, send_ref, grad_ref, kept_ref
):
    core = scalars[0]
    width = own_ref.shape[1]
    for head in range(width // HEAD):
        to = lanes(0, head, width)
        kept_ref[:, to] = inside_ref[:, to] + nn(a_ref[:, to], states_ref[head]) * (1.0 / HEAD)
        taps = taps_ref[:, lanes(RAW, head, width)]
        for first in range(0, PAIR, 64):
            grad = taps[0:1] * kept_ref[first : first + 64, to]
            for j in range(1, TAPS):
                grad = grad + taps[j : j + 1] * kept_ref[first + j : first + j + 64, to]
            grad_ref[first : first + 64, to] = grad.astype(BF16)
    own_ref[...] = grad_ref[pl.ds(pl.multiple_of(core * ROWS, ROWS), ROWS), :]
    send_ref[...] = grad_ref[pl.ds(pl.multiple_of((1 - core) * ROWS, ROWS), ROWS), :]


def join_kernel(scalars, own_ref, other_ref, out_ref):
    width = own_ref.shape[1]
    for core, parts in enumerate(((own_ref, other_ref), (other_ref, own_ref))):

        @pl.when(scalars[0] == core)
        def _():
            for half, part in enumerate(parts):
                out_ref[:, half * width : (half + 1) * width] = part[...]


def per_device(qkv_input, conv_weight, out_cotangent):
    x, g = qkv_input[0], out_cotangent[0]
    width = g.shape[1] // 2
    heads = width // HEAD
    chips = lax.axis_size("zh")
    core, chip, low = lax.axis_index("core"), lax.axis_index("zh"), lax.axis_index("zl")
    scalars = jnp.stack([core, chip]).astype(jnp.int32)
    fitting = (jnp.arange(8 * chips) // (4 * chips) == low // 2).astype(F32)[:, None]
    swap = [(0, 1), (1, 0)]
    line = ("zh", "core")

    def hops(by):
        later = [(2 * c, 2 * (c + by)) for c in range(chips - by)]
        return later + [(2 * (c + by) + 1, 2 * c + 1) for c in range(chips - by)]

    keep, send = call(
        pack_kernel, [((rows, 4 * width), BF16) for rows in (ROWS, ROWS + 16)],
        [pltpu.SemaphoreType.DMA((8,))],
        scalars, x, g, fitting, space=pl.BlockSpec(memory_space=pl.ANY), limit=8,
    )
    (taps,) = call(taps_kernel, [((TAPS, 4 * width), F32)], [], scalars, conv_weight)
    received = lax.ppermute(send, "core", swap)
    padded = [pltpu.VMEM((LONG, HEAD), F32)] * 4
    message = ((heads // 2, HEAD + 4 * EDGE, HEAD), BF16)
    one, two, wrap = call(
        states_kernel, [message, message, ((heads, HEAD + EDGE, HEAD), BF16)],
        padded + [pltpu.VMEM((PAIR, HEAD), BF16)] * 4,
        scalars, keep, received, taps,
    )
    near_one = lax.ppermute(one, line, hops(1))
    near_two = lax.ppermute(two, line, hops(1))
    wrap = lax.ppermute(wrap, line, hops(3))
    spread = lax.axis_size("yx")
    few = width // 2 // spread
    part = -(-TAPS * few // HEAD) * HEAD
    tail = ((16, width), BF16)
    products, fold, rows = call(
        products_kernel,
        [
            ((heads, TAPS, HEAD, HEAD), F32), ((width // 2, 2 * part), BF16),
            ((spread, width // 2), F32),
        ],
        padded, scalars, keep, received, taps, one,
    )
    handed = ((heads // 2, HEAD + 2 * EDGE, HEAD), BF16)
    onward = [pair for pair in hops(1) if pair not in ((0, 2), (2 * chips - 1, 2 * chips - 3))]
    far_one, far_two = (
        lax.ppermute(call(hand_on_kernel, [handed], [], scalars, near, fold)[0], line, onward)
        for near in (near_one, near_two)
    )
    (partner,) = call(
        partner_kernel, [((4, 3 * width), BF16)], [], scalars, near_one, near_two
    )
    partner = lax.ppermute(partner, "core", swap)
    inside, a, left_tail, b_tail, terms, front = call(
        inside_kernel,
        [
            ((EXT, width), F32), ((EXT, width), BF16), tail, tail, ((TAPS, width), F32),
            ((PRE + 8, width), F32),
        ],
        padded + [pltpu.VMEM((EXT, HEAD), BF16)] * 4,
        scalars, keep, received, near_one, near_two, partner, taps,
    )
    states, rows = call(
        terms_kernel, [((heads, HEAD, HEAD), BF16), ((spread, 1, 2 * part), F32)],
        [
            pltpu.VMEM((4, 16, width), F32), pltpu.VMEM((2, 32, width), BF16),
            pltpu.VMEM((TAPS, width), F32), pltpu.VMEM((2 * TAPS * spread, width // 2), F32),
        ],
        scalars, terms, products, a, front, left_tail, b_tail,
        near_one, near_two, far_one, far_two, wrap, taps, fold, rows,
    )
    rows = jnp.sum(lax.all_to_all(rows, "yx", 0, 0, tiled=True), (0, 1)).reshape(2, part)
    rows = jnp.broadcast_to(rows[None, None, :, None], (2, 2, 2, chips, part)).reshape(8 * chips, part)
    own, sent = call(
        input_kernel, [((ROWS, width), BF16)] * 2,
        [pltpu.VMEM((PAIR, width), BF16), pltpu.VMEM((EXT, width), F32)],
        scalars, inside, a, states, taps, rows,
    )
    rows = lax.all_to_all(rows, ("core", "zl", "zh"), 0, 0, tiled=True)
    share = jnp.sum(rows * fitting, 0)[: TAPS * few].reshape(TAPS, few)
    shares = share * (1.0 / (lax.axis_size("zl") * spread))
    other = lax.ppermute(sent, "core", swap)
    (grad,) = call(join_kernel, [((ROWS, 2 * width), BF16)], [], scalars, own, other)
    return grad[None], shares


def solution(mesh):
    dp, seq = mesh.shape["dp"], mesh.shape["seq"]
    fine = Mesh(mesh.devices.reshape(4, dp // 4, seq // 2, 2), ("zl", "yx", "zh", "core"))
    rows = P(("zl", "yx"), ("zh", "core"), None)
    return jax.shard_map(
        per_device, mesh=fine, in_specs=(rows, P(), rows),
        out_specs=(rows, P(None, ("zl", "yx"))), check_vma=False,
    )
```

```python
import jax
import jax.numpy as jnp
from jax import lax
from jax.experimental import pallas as pl
from jax.experimental.pallas import tpu as pltpu
from jax.sharding import Mesh
from jax.sharding import PartitionSpec as P

HEAD = 128
TAPS = 4
ROWS = 128
PAIR = 2 * ROWS
EXT = PAIR + 16
PRE = 8
LONG = PRE + PAIR + 8
EDGE = 8
F32 = jnp.float32
BF16 = jnp.bfloat16
LEFT, A, B, RAW = range(4)
VMEM = pl.BlockSpec(memory_space=pltpu.VMEM)
SMEM = pl.BlockSpec(memory_space=pltpu.SMEM)


def call(kernel, shapes, scratch, scalars, *arrays, space=VMEM, limit=16):
    return pl.pallas_call(
        kernel,
        out_shape=[jax.ShapeDtypeStruct(s, t) for s, t in shapes],
        in_specs=[SMEM] + [space] * len(arrays),
        out_specs=[VMEM] * len(shapes),
        scratch_shapes=scratch,
        compiler_params=pltpu.CompilerParams(vmem_limit_bytes=limit * 1024 * 1024),
    )(scalars, *arrays)


def nt(a, b):
    return lax.dot_general(a, b, (((1,), (1,)), ((), ())), preferred_element_type=F32)


def tn(a, b):
    return lax.dot_general(a, b, (((0,), (0,)), ((), ())), preferred_element_type=F32)


def nn(a, b):
    return lax.dot_general(a, b, (((1,), (0,)), ((), ())), preferred_element_type=F32)


def lanes(group, head, width):
    return slice(group * width + head * HEAD, group * width + (head + 1) * HEAD)


def fill_edges(core, keep_ref, send_ref):
    width = keep_ref.shape[1] // 4
    edge = pl.ds(pl.multiple_of(core * (ROWS - 16), 16), 16)
    none = jnp.zeros((12, width), F32)
    for slot, (first, last) in enumerate(((LEFT, LEFT), (A, A), (B, RAW), (RAW, RAW))):
        zero = keep_ref[edge, first * width : (first + 1) * width].astype(F32)[0:4]
        one = keep_ref[edge, last * width : (last + 1) * width].astype(F32)[12:16]
        rows = jnp.concatenate([jnp.where(core == 1, one, zero), none], 0)
        send_ref[ROWS : ROWS + 16, slot * width : (slot + 1) * width] = rows.astype(BF16)


def pack_kernel(scalars, x_ref, g_ref, before_ref, keep_ref, send_ref, sems):
    core = scalars[0]
    width = keep_ref.shape[1] // 4
    of_core = (
        ((x_ref, 3), (g_ref, 1), (x_ref, 5), (x_ref, 1)),
        ((x_ref, 0), (x_ref, 4), (g_ref, 0), (x_ref, 2)),
    )

    def fill(mine):
        copies = []

        def copy(source_ref, group, out_ref, slot):
            lanes_in = slice(group * width, (group + 1) * width)
            lanes_out = slice(slot * width, (slot + 1) * width)
            copies.append(
                pltpu.make_async_copy(
                    source_ref.at[:, lanes_in], out_ref.at[0:ROWS, lanes_out], sems.at[len(copies)]
                )
            )

        for slot, (source_ref, group) in enumerate(of_core[1 - mine]):
            copy(source_ref, group, send_ref, slot)
        for slot, (source_ref, group) in enumerate(of_core[mine]):
            copy(source_ref, group, keep_ref, slot)
        for each in copies:
            each.start()
        for each in copies:
            each.wait()

    @pl.when(core == 0)
    def _():
        fill(0)

    @pl.when(core == 1)
    def _():
        fill(1)

    fill_edges(core, keep_ref, send_ref)


def taps_kernel(scalars, w_ref, taps_ref):
    width = taps_ref.shape[1] // 4
    row = lax.broadcasted_iota(jnp.int32, (TAPS, width), 0)
    unit = jnp.where(row == 0, 1.0, 0.0).astype(F32)
    for core, groups in enumerate(((3, None, 5, 1), (0, 4, None, 2))):

        @pl.when(scalars[0] == core)
        def _():
            for slot, group in enumerate(groups):
                part = unit if group is None else w_ref[:, group * width : (group + 1) * width]
                taps_ref[:, slot * width : (slot + 1) * width] = part


def gather_rows(core, keep_ref, received_ref, at, padded_ref):
    own = pl.ds(pl.multiple_of(PRE + core * ROWS, 8), ROWS)
    other = pl.ds(pl.multiple_of(PRE + (1 - core) * ROWS, 8), ROWS)
    padded_ref[own, :] = keep_ref[:, at].astype(F32)
    padded_ref[other, :] = received_ref[0:ROWS, at].astype(F32)


def convolved(padded_ref, taps, start, count):
    total = taps[0:1] * padded_ref[start : start + count, :]
    for j in range(1, TAPS):
        total = total + taps[j : j + 1] * padded_ref[start - j : start - j + count, :]
    return total


def half_of(one_ref, two_ref, head):
    first = one_ref.shape[0]
    return (one_ref, head) if head < first else (two_ref, head - first)


def states_kernel(scalars, keep_ref, received_ref, taps_ref, message_ref, *scratch, begin=0):
    core, chip = scalars[0], scalars[1]
    width = keep_ref.shape[1] // 4
    padded_refs, value_refs = scratch[:4], scratch[4:]
    for ref in padded_refs:
        ref[0:PRE, :] = jnp.zeros((PRE, HEAD), F32)
    row = lax.broadcasted_iota(jnp.int32, (ROWS, HEAD), 0)
    kept_rows = (row >= TAPS - 1) | (chip == 0)
    first_rows = jnp.where(chip == 0, 0.0, 1.0)
    for place in range(message_ref.shape[0]):
        head = begin + place
        firsts, lasts = [], []
        for turn, group in enumerate((LEFT, B)):
            padded_ref = padded_refs[(2 * head + turn) % 4]
            value_ref = value_refs[(2 * head + turn) % 4]
            at = lanes(group, head, width)
            gather_rows(core, keep_ref, received_ref, at, padded_ref)
            taps = taps_ref[:, at]
            for first in (0, ROWS):
                total = convolved(padded_ref, taps, PRE + first, ROWS)
                if group == LEFT and first == 0:
                    total = jnp.where(kept_rows, total, 0.0)
                value_ref[first : first + ROWS, :] = total.astype(BF16)
            front = padded_ref[PRE : PRE + 4, :]
            firsts.append(front * first_rows if group == LEFT else front)
            lasts.append(padded_ref[PRE + PAIR - 4 : PRE + PAIR, :])
        left, right = value_refs[(2 * head) % 4], value_refs[(2 * head + 1) % 4]
        message_ref[place, 0:HEAD, :] = tn(right[...], left[...]).astype(BF16)
        third = jnp.where(
            core == 0,
            received_ref[ROWS - 16 : ROWS, lanes(RAW, head, width)].astype(F32)[12:16],
            received_ref[0:16, lanes(A, head, width)].astype(F32)[0:4],
        )
        others = [
            received_ref[ROWS : ROWS + 16, lanes(slot, head, width)].astype(F32)[0:4] for slot in range(3)
        ]
        message_ref[place, HEAD:, :] = jnp.concatenate([*firsts, *lasts, third, *others], 0).astype(BF16)


def second_states_kernel(
    scalars, keep_ref, received_ref, taps_ref, one_ref, after_ref, two_ref, wrap_ref, *scratch
):
    states_kernel(scalars, keep_ref, received_ref, taps_ref, two_ref, *scratch, begin=one_ref.shape[0])
    for head in range(wrap_ref.shape[0]):
        message_ref, at = half_of(one_ref, two_ref, head)
        wrap_ref[head, 0:HEAD, :] = message_ref[at, 0:HEAD, :]
        edges = message_ref[at, HEAD : HEAD + 2 * EDGE, :].astype(F32)
        edges = jnp.where(scalars[0] == 0, edges[EDGE:], edges[:EDGE])
        wrap_ref[head, HEAD:, :] = edges.astype(BF16)


def partner_kernel(scalars, near_one_ref, near_two_ref, out_ref):
    width = out_ref.shape[1] // 3
    for head in range(width // HEAD):
        near_ref, at = half_of(near_one_ref, near_two_ref, head)
        rows = near_ref[at, HEAD + 2 * EDGE :, :].astype(F32)
        for slot in range(3):
            out_ref[:, lanes(slot, head, width)] = rows[4 * slot + 4 : 4 * slot + 8].astype(BF16)


def hand_on_kernel(scalars, message_ref, after_ref, out_ref):
    out_ref[...] = message_ref[:, 0 : out_ref.shape[1], :]


def products_kernel(
    scalars, keep_ref, received_ref, taps_ref, after_ref, products_ref, fold_ref, rows_ref, *padded_refs
):
    core = scalars[0]
    width = keep_ref.shape[1] // 4
    for ref in padded_refs:
        ref[0:PRE, :] = jnp.zeros((PRE, HEAD), F32)
    row = lax.broadcasted_iota(jnp.int32, (PAIR, HEAD), 0)
    for head in range(width // HEAD):
        a_ref, raw_ref = (padded_refs[(2 * head + k) % 4] for k in range(2))
        at = lanes(A, head, width)
        gather_rows(core, keep_ref, received_ref, at, a_ref)
        gather_rows(core, keep_ref, received_ref, lanes(RAW, head, width), raw_ref)
        a = convolved(a_ref, taps_ref[:, at], PRE, PAIR)
        a = jnp.where(row >= TAPS - 1, a, 0.0).astype(BF16)
        for j in range(TAPS):
            shifted = raw_ref[PRE - j : PRE - j + PAIR, :].astype(BF16)
            products_ref[head, j] = tn(a, shifted) * (1.0 / HEAD)
    few = width // 2 // rows_ref.shape[0]
    place = lax.broadcasted_iota(jnp.int32, fold_ref.shape, 1)
    column = lax.broadcasted_iota(jnp.int32, fold_ref.shape, 0)
    place = lax.rem(place, fold_ref.shape[1] // 2)
    fits = (lax.rem(column, few) == lax.rem(place, few)) & (place < TAPS * few)
    fold_ref[...] = jnp.where(fits, 1.0, 0.0).astype(BF16)
    device = lax.broadcasted_iota(jnp.int32, rows_ref.shape, 0) * few
    column = lax.broadcasted_iota(jnp.int32, rows_ref.shape, 1)
    rows_ref[...] = jnp.where((column >= device) & (column < device + few), 1.0, 0.0)


def inside_kernel(
    scalars, keep_ref, received_ref, near_one_ref, near_two_ref, other_ref, taps_ref,
    kept_ref, a_ref, left_tail_ref, b_tail_ref, terms_ref, front_ref, *scratch,
):
    core = scalars[0]
    width = keep_ref.shape[1] // 4
    padded_refs, value_refs = scratch[:4], scratch[4:]
    other = other_ref[...].astype(F32)
    row = lax.broadcasted_iota(jnp.int32, (EXT, EXT), 0)
    column = lax.broadcasted_iota(jnp.int32, (EXT, EXT), 1)
    causal = jnp.where(column <= row, 1.0 / HEAD, 0.0)
    reverse = jnp.where(
        (column >= row) & (column < PAIR),
        1.0 / HEAD,
        jnp.where((column >= PAIR) & (column < row), -1.0 / HEAD, 0.0),
    )
    mask = jnp.where(core == 0, causal, reverse)
    none = jnp.zeros((4, HEAD), F32)
    tail_row = lax.broadcasted_iota(jnp.int32, (16, HEAD), 0)
    tail_used = (tail_row < TAPS - 1) & (core == 1)
    turn = 0
    for head in range(width // HEAD):
        to = lanes(0, head, width)
        values = []
        near_ref, half = half_of(near_one_ref, near_two_ref, head)
        near = near_ref[half, HEAD:, :].astype(F32)
        first, last, third = near[0:EDGE], near[EDGE : 2 * EDGE], near[2 * EDGE : 2 * EDGE + 4]
        partner = [other[:, lanes(slot, head, width)] for slot in range(3)]
        befores = zip((last[0:4], third, last[4:8], third), (partner[0], partner[1], partner[1], partner[2]))
        afters = zip((partner[0], partner[1], partner[2], third), (first[0:4], third, first[4:8], third))
        befores, afters = ([jnp.where(core == 0, *pair) for pair in pairs] for pairs in (befores, afters))
        for group in (LEFT, A, B, RAW):
            padded_ref = padded_refs[turn % 4]
            value_ref = value_refs[turn % 4]
            turn += 1
            at = lanes(group, head, width)
            gather_rows(core, keep_ref, received_ref, at, padded_ref)
            padded_ref[0:PRE, :] = jnp.concatenate([none, befores[group]], 0)
            padded_ref[PRE + PAIR : LONG, :] = jnp.concatenate([afters[group], none], 0)
            if group == RAW:
                raw_ref = padded_ref
                continue
            taps = taps_ref[:, at]
            for first in (0, ROWS):
                total = convolved(padded_ref, taps, PRE + first, ROWS)
                value_ref[first : first + ROWS, :] = total.astype(BF16)
            tail = convolved(padded_ref, taps, PRE + PAIR, 8)
            tail = jnp.concatenate([tail, jnp.zeros((8, HEAD), F32)], 0)
            value_ref[PAIR:EXT, :] = tail.astype(BF16)
            if group != A:
                tail_ref = left_tail_ref if group == LEFT else b_tail_ref
                tail_ref[:, to] = jnp.where(tail_used, tail, 0.0).astype(BF16)
            values.append(value_ref)
        left, a, b = (ref[...] for ref in values)
        a_ref[:, to] = a
        scores = (nt(a, b) * mask).astype(BF16)
        kept_ref[:, to] = nn(scores, left)
        front_ref[:, to] = raw_ref[0 : PRE + 8, :]
        sums = [jnp.zeros((8, HEAD), F32)] * TAPS
        for first in range(0, PAIR, 64):
            kept = kept_ref[first : first + 64, to]
            for j in range(TAPS):
                start = PRE + first - j
                term = kept * raw_ref[start : start + 64, :]
                sums[j] = sums[j] + jnp.sum(term.reshape(8, 8, HEAD), 0)
        terms_ref[:, to] = jnp.concatenate([jnp.sum(s, 0, keepdims=True) for s in sums], 0)


def terms_kernel(
    scalars, terms_ref, products_ref, a_ref, front_ref, left_tail_ref, b_tail_ref,
    near_one_ref, near_two_ref, far_one_ref, far_two_ref, wrap_ref, taps_ref, fold_ref, rows_ref,
    states_ref, shares_ref, edge_ref, seam_ref, total_ref, stack_ref,
):
    core = scalars[0]
    heads, width = products_ref.shape[0], terms_ref.shape[1]
    none = jnp.zeros((8, HEAD), F32)
    for head in range(heads):
        to = lanes(0, head, width)
        near_ref, at = half_of(near_one_ref, near_two_ref, head)
        far_ref, _ = half_of(far_one_ref, far_two_ref, head)
        near, far = (r[at, HEAD : HEAD + 2 * EDGE, :].astype(F32) for r in (near_ref, far_ref))
        wrap = wrap_ref[head, HEAD:, :].astype(F32)
        near = jnp.where(core == 0, near[0:EDGE], near[EDGE : 2 * EDGE])
        first, last = far[0:EDGE], far[EDGE : 2 * EDGE]
        for turn, (zero, one) in enumerate((((last, near), (near, first)), ((wrap, first), (last, wrap)))):
            before, after = (jnp.where(core == 0, *pair) for pair in zip(zero, one))
            for slot, at in enumerate((slice(0, 4), slice(4, 8))):
                edge_ref[2 * slot + turn, 0:8, to] = jnp.concatenate([before[at], after[at]], 0)
                edge_ref[2 * slot + turn, 8:16, to] = none
    row = lax.broadcasted_iota(jnp.int32, (8, width), 0)
    for slot, group, tail_ref in ((0, LEFT, left_tail_ref), (1, B, b_tail_ref)):
        taps = taps_ref[:, group * width : (group + 1) * width]
        rows = [convolved(edge_ref.at[2 * slot + turn], taps, 4, 8) for turn in range(2)]
        rows = [jnp.where(row < TAPS - 1, total, 0.0) for total in rows]
        seam_ref[slot, 0:16, :] = jnp.concatenate(rows, 0).astype(BF16)
        seam_ref[slot, 16:32, :] = tail_ref[...]
    every = [(head, lanes(0, head, width)) for head in range(heads)]
    seams = [tn(seam_ref[1, :, to], seam_ref[0, :, to]) for _, to in every]
    states = []
    for (head, _), seam in zip(every, seams):
        near_ref, at = half_of(near_one_ref, near_two_ref, head)
        far_ref, _ = half_of(far_one_ref, far_two_ref, head)
        near, far = (r[at, 0:HEAD, :].astype(F32) for r in (near_ref, far_ref))
        wrap = wrap_ref[head, 0:HEAD, :].astype(F32)
        states.append((near + far + (wrap + seam)).astype(BF16))
    fronts = [nn(a_ref[0:16, to], state) for (_, to), state in zip(every, states)]
    row = lax.broadcasted_iota(jnp.int32, (8, HEAD), 0)
    for (head, to), state, front in zip(every, states, fronts):
        states_ref[head] = state
        state = state.astype(F32)
        front = jnp.where(row < TAPS - 1, front[0:8] * (1.0 / HEAD), 0.0)
        sums = []
        for j in range(TAPS):
            product = (state * products_ref[head, j]).reshape(HEAD // 8, 8, HEAD)
            total = jnp.sum(product, 0) + front * front_ref[PRE - j : PRE - j + 8, to]
            sums.append(jnp.sum(total, 0, keepdims=True))
        total_ref[:, to] = terms_ref[:, to] + jnp.concatenate(sums, 0)
    half = width // 2
    spread = rows_ref.shape[0]
    fitting = rows_ref[...]
    for part in range(2):
        for j in range(TAPS):
            at = (part * TAPS + j) * spread
            line = total_ref[j : j + 1, part * half : (part + 1) * half]
            stack_ref[at : at + spread, :] = fitting * line
    folded = nn(stack_ref[...].astype(BF16), fold_ref[...])
    few = half // spread
    place = lax.broadcasted_iota(jnp.int32, (spread, fold_ref.shape[1]), 1)
    gathered = jnp.zeros((spread, fold_ref.shape[1]), F32)
    for part in range(2):
        for j in range(TAPS):
            at = (part * TAPS + j) * spread
            begin = part * (fold_ref.shape[1] // 2) + j * few
            here = (place >= begin) & (place < begin + few)
            gathered = gathered + jnp.where(here, folded[at : at + spread], 0.0)
    shares_ref[...] = gathered.reshape(shares_ref.shape)


def input_kernel(
    scalars, inside_ref, a_ref, states_ref, taps_ref, after_ref, own_ref, send_ref, grad_ref, kept_ref
):
    core = scalars[0]
    width = own_ref.shape[1]
    for head in range(width // HEAD):
        to = lanes(0, head, width)
        kept_ref[:, to] = inside_ref[:, to] + nn(a_ref[:, to], states_ref[head]) * (1.0 / HEAD)
        taps = taps_ref[:, lanes(RAW, head, width)]
        for first in range(0, PAIR, 64):
            grad = taps[0:1] * kept_ref[first : first + 64, to]
            for j in range(1, TAPS):
                grad = grad + taps[j : j + 1] * kept_ref[first + j : first + j + 64, to]
            grad_ref[first : first + 64, to] = grad.astype(BF16)
    own_ref[...] = grad_ref[pl.ds(pl.multiple_of(core * ROWS, ROWS), ROWS), :]
    send_ref[...] = grad_ref[pl.ds(pl.multiple_of((1 - core) * ROWS, ROWS), ROWS), :]


def join_kernel(scalars, own_ref, other_ref, fitting_ref, out_ref, fitting_out_ref):
    fitting_out_ref[...] = fitting_ref[...]
    width = own_ref.shape[1]
    for core, parts in enumerate(((own_ref, other_ref), (other_ref, own_ref))):

        @pl.when(scalars[0] == core)
        def _():
            for half, part in enumerate(parts):
                out_ref[:, half * width : (half + 1) * width] = part[...]


def per_device(qkv_input, conv_weight, out_cotangent):
    x, g = qkv_input[0], out_cotangent[0]
    width = g.shape[1] // 2
    heads = width // HEAD
    chips = lax.axis_size("zh")
    core, chip, low = lax.axis_index("core"), lax.axis_index("zh"), lax.axis_index("zl")
    scalars = jnp.stack([core, chip]).astype(jnp.int32)
    fitting = (jnp.arange(8 * chips) // (4 * chips) == low // 2).astype(F32)[:, None]
    swap = [(0, 1), (1, 0)]
    line = ("zh", "core")

    def hops(by):
        later = [(2 * c, 2 * (c + by)) for c in range(chips - by)]
        return later + [(2 * (c + by) + 1, 2 * c + 1) for c in range(chips - by)]

    keep, send = call(
        pack_kernel, [((rows, 4 * width), BF16) for rows in (ROWS, ROWS + 16)],
        [pltpu.SemaphoreType.DMA((8,))],
        scalars, *(pltpu.with_memory_space_constraint(each, pltpu.HBM) for each in (x, g)), fitting,
        space=pl.BlockSpec(memory_space=pl.ANY), limit=8,
    )
    (taps,) = call(taps_kernel, [((TAPS, 4 * width), F32)], [], scalars, conv_weight)
    received = lax.ppermute(send, "core", swap)
    padded = [pltpu.VMEM((LONG, HEAD), F32)] * 4
    message, second = (((many, HEAD + 4 * EDGE, HEAD), BF16) for many in (6 * heads // 10, heads - 6 * heads // 10))
    buffers = padded + [pltpu.VMEM((PAIR, HEAD), BF16)] * 4
    (one,) = call(states_kernel, [message], buffers, scalars, keep, received, taps)
    near_one = lax.ppermute(one, line, hops(1))
    spread = lax.axis_size("yx")
    few = width // 2 // spread
    part = -(-TAPS * few // HEAD) * HEAD
    tail = ((16, width), BF16)
    products, fold, rows = call(
        products_kernel,
        [
            ((heads, TAPS, HEAD, HEAD), F32), ((width // 2, 2 * part), BF16),
            ((spread, width // 2), F32),
        ],
        padded, scalars, keep, received, taps, one,
    )
    two, wrap = call(
        second_states_kernel, [second, ((heads, HEAD + EDGE, HEAD), BF16)], buffers,
        scalars, keep, received, taps, one, fold,
    )
    near_two = lax.ppermute(two, line, hops(1))
    wrap = lax.ppermute(wrap, line, hops(3))
    onward = [pair for pair in hops(1) if pair not in ((0, 2), (2 * chips - 1, 2 * chips - 3))]
    far_one, far_two = (
        lax.ppermute(call(
            hand_on_kernel, [((near.shape[0], HEAD + 2 * EDGE, HEAD), BF16)], [], scalars, near, fold
        )[0], line, onward)
        for near in (near_one, near_two)
    )
    (partner,) = call(
        partner_kernel, [((4, 3 * width), BF16)], [], scalars, near_one, near_two
    )
    partner = lax.ppermute(partner, "core", swap)
    inside, a, left_tail, b_tail, terms, front = call(
        inside_kernel,
        [
            ((EXT, width), F32), ((EXT, width), BF16), tail, tail, ((TAPS, width), F32),
            ((PRE + 8, width), F32),
        ],
        padded + [pltpu.VMEM((EXT, HEAD), BF16)] * 4,
        scalars, keep, received, near_one, near_two, partner, taps,
    )
    states, rows = call(
        terms_kernel, [((heads, HEAD, HEAD), BF16), ((spread, 1, 2 * part), F32)],
        [
            pltpu.VMEM((4, 16, width), F32), pltpu.VMEM((2, 32, width), BF16),
            pltpu.VMEM((TAPS, width), F32), pltpu.VMEM((2 * TAPS * spread, width // 2), F32),
        ],
        scalars, terms, products, a, front, left_tail, b_tail,
        near_one, near_two, far_one, far_two, wrap, taps, fold, rows,
    )
    rows = jnp.sum(lax.all_to_all(rows, "yx", 0, 0, tiled=True), (0, 1)).reshape(2, part)
    rows = jnp.broadcast_to(rows[None, None, :, None], (2, 2, 2, chips, part)).reshape(8 * chips, part)
    own, sent = call(
        input_kernel, [((ROWS, width), BF16)] * 2,
        [pltpu.VMEM((PAIR, width), BF16), pltpu.VMEM((EXT, width), F32)],
        scalars, inside, a, states, taps, rows,
    )
    rows = lax.all_to_all(rows, ("core", "zl", "zh"), 0, 0, tiled=True)
    other = lax.ppermute(sent, "core", swap)
    grad, fitting = call(
        join_kernel, [((ROWS, 2 * width), BF16), (fitting.shape, F32)], [], scalars, own, other, fitting
    )
    share = jnp.sum(rows * fitting, 0)[: TAPS * few].reshape(TAPS, few)
    return grad[None], share * (1.0 / (lax.axis_size("zl") * spread))


def solution(mesh):
    dp, seq = mesh.shape["dp"], mesh.shape["seq"]
    fine = Mesh(mesh.devices.reshape(4, dp // 4, seq // 2, 2), ("zl", "yx", "zh", "core"))
    rows = P(("zl", "yx"), ("zh", "core"), None)
    return jax.shard_map(
        per_device, mesh=fine, in_specs=(rows, P(), rows),
        out_specs=(rows, P(None, ("zl", "yx"))), check_vma=False,
    )
```

```python
import jax
import jax.numpy as jnp
from jax import lax
from jax.experimental import pallas as pl
from jax.experimental.pallas import tpu as pltpu
from jax.sharding import Mesh
from jax.sharding import PartitionSpec as P

HEAD = 128
TAPS = 4
ROWS = 128
PAIR = 2 * ROWS
EXT = PAIR + 16
PRE = 8
LONG = PRE + PAIR + 8
EDGE = 8
F32 = jnp.float32
BF16 = jnp.bfloat16
LEFT, A, B, RAW = range(4)
VMEM = pl.BlockSpec(memory_space=pltpu.VMEM)
SMEM = pl.BlockSpec(memory_space=pltpu.SMEM)


def call(kernel, shapes, scratch, scalars, *arrays, space=VMEM, limit=16):
    return pl.pallas_call(
        kernel,
        out_shape=[jax.ShapeDtypeStruct(s, t) for s, t in shapes],
        in_specs=[SMEM] + [space] * len(arrays),
        out_specs=[VMEM] * len(shapes),
        scratch_shapes=scratch,
        compiler_params=pltpu.CompilerParams(vmem_limit_bytes=limit * 1024 * 1024),
    )(scalars, *arrays)


def nt(a, b):
    return lax.dot_general(a, b, (((1,), (1,)), ((), ())), preferred_element_type=F32)


def tn(a, b):
    return lax.dot_general(a, b, (((0,), (0,)), ((), ())), preferred_element_type=F32)


def nn(a, b):
    return lax.dot_general(a, b, (((1,), (0,)), ((), ())), preferred_element_type=F32)


def lanes(group, head, width):
    return slice(group * width + head * HEAD, group * width + (head + 1) * HEAD)


def fill_edges(core, keep_ref, send_ref):
    width = keep_ref.shape[1] // 4
    edge = pl.ds(pl.multiple_of(core * (ROWS - 16), 16), 16)
    none = jnp.zeros((12, width), F32)
    for slot, (first, last) in enumerate(((LEFT, LEFT), (A, A), (B, RAW), (RAW, RAW))):
        zero = keep_ref[edge, first * width : (first + 1) * width].astype(F32)[0:4]
        one = keep_ref[edge, last * width : (last + 1) * width].astype(F32)[12:16]
        rows = jnp.concatenate([jnp.where(core == 1, one, zero), none], 0)
        send_ref[ROWS : ROWS + 16, slot * width : (slot + 1) * width] = rows.astype(BF16)


def pack_kernel(scalars, x_ref, g_ref, before_ref, keep_ref, send_ref, sems):
    core = scalars[0]
    width = keep_ref.shape[1] // 4
    of_core = (
        ((x_ref, 3), (g_ref, 1), (x_ref, 5), (x_ref, 1)),
        ((x_ref, 0), (x_ref, 4), (g_ref, 0), (x_ref, 2)),
    )

    def fill(mine):
        copies = []

        def copy(source_ref, group, out_ref, slot):
            lanes_in = slice(group * width, (group + 1) * width)
            lanes_out = slice(slot * width, (slot + 1) * width)
            copies.append(
                pltpu.make_async_copy(
                    source_ref.at[:, lanes_in], out_ref.at[0:ROWS, lanes_out], sems.at[len(copies)]
                )
            )

        for slot, (source_ref, group) in enumerate(of_core[1 - mine]):
            copy(source_ref, group, send_ref, slot)
        for slot, (source_ref, group) in enumerate(of_core[mine]):
            copy(source_ref, group, keep_ref, slot)
        for each in copies:
            each.start()
        for each in copies:
            each.wait()

    @pl.when(core == 0)
    def _():
        fill(0)

    @pl.when(core == 1)
    def _():
        fill(1)

    fill_edges(core, keep_ref, send_ref)


def taps_kernel(scalars, w_ref, taps_ref):
    width = taps_ref.shape[1] // 4
    row = lax.broadcasted_iota(jnp.int32, (TAPS, width), 0)
    unit = jnp.where(row == 0, 1.0, 0.0).astype(F32)
    for core, groups in enumerate(((3, None, 5, 1), (0, 4, None, 2))):

        @pl.when(scalars[0] == core)
        def _():
            for slot, group in enumerate(groups):
                part = unit if group is None else w_ref[:, group * width : (group + 1) * width]
                taps_ref[:, slot * width : (slot + 1) * width] = part


def gather_rows(core, keep_ref, received_ref, at, padded_ref):
    own = pl.ds(pl.multiple_of(PRE + core * ROWS, 8), ROWS)
    other = pl.ds(pl.multiple_of(PRE + (1 - core) * ROWS, 8), ROWS)
    padded_ref[own, :] = keep_ref[:, at].astype(F32)
    padded_ref[other, :] = received_ref[0:ROWS, at].astype(F32)


def convolved(padded_ref, taps, start, count):
    total = taps[0:1] * padded_ref[start : start + count, :]
    for j in range(1, TAPS):
        total = total + taps[j : j + 1] * padded_ref[start - j : start - j + count, :]
    return total


def half_of(one_ref, two_ref, head):
    first = one_ref.shape[0]
    return (one_ref, head) if head < first else (two_ref, head - first)


def states_kernel(scalars, keep_ref, received_ref, taps_ref, message_ref, *scratch, begin=0):
    core, chip = scalars[0], scalars[1]
    width = keep_ref.shape[1] // 4
    padded_refs, value_refs = scratch[:4], scratch[4:]
    for ref in padded_refs:
        ref[0:PRE, :] = jnp.zeros((PRE, HEAD), F32)
    row = lax.broadcasted_iota(jnp.int32, (ROWS, HEAD), 0)
    kept_rows = (row >= TAPS - 1) | (chip == 0)
    first_rows = jnp.where(chip == 0, 0.0, 1.0)
    for place in range(message_ref.shape[0]):
        head = begin + place
        firsts, lasts = [], []
        for turn, group in enumerate((LEFT, B)):
            padded_ref = padded_refs[(2 * head + turn) % 4]
            value_ref = value_refs[(2 * head + turn) % 4]
            at = lanes(group, head, width)
            gather_rows(core, keep_ref, received_ref, at, padded_ref)
            taps = taps_ref[:, at]
            for first in (0, ROWS):
                total = convolved(padded_ref, taps, PRE + first, ROWS)
                if group == LEFT and first == 0:
                    total = jnp.where(kept_rows, total, 0.0)
                value_ref[first : first + ROWS, :] = total.astype(BF16)
            front = padded_ref[PRE : PRE + 4, :]
            firsts.append(front * first_rows if group == LEFT else front)
            lasts.append(padded_ref[PRE + PAIR - 4 : PRE + PAIR, :])
        left, right = value_refs[(2 * head) % 4], value_refs[(2 * head + 1) % 4]
        message_ref[place, 0:HEAD, :] = tn(right[...], left[...]).astype(BF16)
        third = jnp.where(
            core == 0,
            received_ref[ROWS - 16 : ROWS, lanes(RAW, head, width)].astype(F32)[12:16],
            received_ref[0:16, lanes(A, head, width)].astype(F32)[0:4],
        )
        others = [
            received_ref[ROWS : ROWS + 16, lanes(slot, head, width)].astype(F32)[0:4] for slot in range(3)
        ]
        message_ref[place, HEAD:, :] = jnp.concatenate([*firsts, *lasts, third, *others], 0).astype(BF16)


def second_states_kernel(
    scalars, keep_ref, received_ref, taps_ref, one_ref, after_ref, two_ref, *scratch
):
    states_kernel(scalars, keep_ref, received_ref, taps_ref, two_ref, *scratch, begin=one_ref.shape[0])


def wrap_kernel(scalars, one_ref, two_ref, wrap_ref):
    for head in range(wrap_ref.shape[0]):
        message_ref, at = half_of(one_ref, two_ref, head)
        wrap_ref[head, 0:HEAD, :] = message_ref[at, 0:HEAD, :]
        edges = message_ref[at, HEAD : HEAD + 2 * EDGE, :].astype(F32)
        edges = jnp.where(scalars[0] == 0, edges[EDGE:], edges[:EDGE])
        wrap_ref[head, HEAD:, :] = edges.astype(BF16)


def partner_kernel(scalars, near_one_ref, near_two_ref, out_ref):
    width = out_ref.shape[1] // 3
    for head in range(width // HEAD):
        near_ref, at = half_of(near_one_ref, near_two_ref, head)
        rows = near_ref[at, HEAD + 2 * EDGE :, :].astype(F32)
        for slot in range(3):
            out_ref[:, lanes(slot, head, width)] = rows[4 * slot + 4 : 4 * slot + 8].astype(BF16)


def hand_on_kernel(scalars, message_ref, after_ref, out_ref):
    out_ref[...] = message_ref[:, 0 : out_ref.shape[1], :]


def products_kernel(
    scalars, keep_ref, received_ref, taps_ref, after_ref, products_ref, fold_ref, rows_ref, *padded_refs
):
    core = scalars[0]
    width = keep_ref.shape[1] // 4
    for ref in padded_refs:
        ref[0:PRE, :] = jnp.zeros((PRE, HEAD), F32)
    row = lax.broadcasted_iota(jnp.int32, (PAIR, HEAD), 0)
    for head in range(width // HEAD):
        a_ref, raw_ref = (padded_refs[(2 * head + k) % 4] for k in range(2))
        at = lanes(A, head, width)
        gather_rows(core, keep_ref, received_ref, at, a_ref)
        gather_rows(core, keep_ref, received_ref, lanes(RAW, head, width), raw_ref)
        a = convolved(a_ref, taps_ref[:, at], PRE, PAIR)
        a = jnp.where(row >= TAPS - 1, a, 0.0).astype(BF16)
        for j in range(TAPS):
            shifted = raw_ref[PRE - j : PRE - j + PAIR, :].astype(BF16)
            products_ref[head, j] = tn(a, shifted) * (1.0 / HEAD)
    few = width // 2 // rows_ref.shape[0]
    place = lax.broadcasted_iota(jnp.int32, fold_ref.shape, 1)
    column = lax.broadcasted_iota(jnp.int32, fold_ref.shape, 0)
    place = lax.rem(place, fold_ref.shape[1] // 2)
    fits = (lax.rem(column, few) == lax.rem(place, few)) & (place < TAPS * few)
    fold_ref[...] = jnp.where(fits, 1.0, 0.0).astype(BF16)
    device = lax.broadcasted_iota(jnp.int32, rows_ref.shape, 0) * few
    column = lax.broadcasted_iota(jnp.int32, rows_ref.shape, 1)
    rows_ref[...] = jnp.where((column >= device) & (column < device + few), 1.0, 0.0)


def inside_kernel(
    scalars, keep_ref, received_ref, near_one_ref, near_two_ref, other_ref, taps_ref,
    kept_ref, a_ref, left_tail_ref, b_tail_ref, terms_ref, front_ref, *scratch,
):
    core = scalars[0]
    width = keep_ref.shape[1] // 4
    padded_refs, value_refs = scratch[:4], scratch[4:]
    other = other_ref[...].astype(F32)
    row = lax.broadcasted_iota(jnp.int32, (EXT, EXT), 0)
    column = lax.broadcasted_iota(jnp.int32, (EXT, EXT), 1)
    causal = jnp.where(column <= row, 1.0 / HEAD, 0.0)
    reverse = jnp.where(
        (column >= row) & (column < PAIR),
        1.0 / HEAD,
        jnp.where((column >= PAIR) & (column < row), -1.0 / HEAD, 0.0),
    )
    mask = jnp.where(core == 0, causal, reverse)
    none = jnp.zeros((4, HEAD), F32)
    tail_row = lax.broadcasted_iota(jnp.int32, (16, HEAD), 0)
    tail_used = (tail_row < TAPS - 1) & (core == 1)
    turn = 0
    for head in range(width // HEAD):
        to = lanes(0, head, width)
        values = []
        near_ref, half = half_of(near_one_ref, near_two_ref, head)
        near = near_ref[half, HEAD:, :].astype(F32)
        first, last, third = near[0:EDGE], near[EDGE : 2 * EDGE], near[2 * EDGE : 2 * EDGE + 4]
        partner = [other[:, lanes(slot, head, width)] for slot in range(3)]
        befores = zip((last[0:4], third, last[4:8], third), (partner[0], partner[1], partner[1], partner[2]))
        afters = zip((partner[0], partner[1], partner[2], third), (first[0:4], third, first[4:8], third))
        befores, afters = ([jnp.where(core == 0, *pair) for pair in pairs] for pairs in (befores, afters))
        for group in (LEFT, A, B, RAW):
            padded_ref = padded_refs[turn % 4]
            value_ref = value_refs[turn % 4]
            turn += 1
            at = lanes(group, head, width)
            gather_rows(core, keep_ref, received_ref, at, padded_ref)
            padded_ref[0:PRE, :] = jnp.concatenate([none, befores[group]], 0)
            padded_ref[PRE + PAIR : LONG, :] = jnp.concatenate([afters[group], none], 0)
            if group == RAW:
                raw_ref = padded_ref
                continue
            taps = taps_ref[:, at]
            for first in (0, ROWS):
                total = convolved(padded_ref, taps, PRE + first, ROWS)
                value_ref[first : first + ROWS, :] = total.astype(BF16)
            tail = convolved(padded_ref, taps, PRE + PAIR, 8)
            tail = jnp.concatenate([tail, jnp.zeros((8, HEAD), F32)], 0)
            value_ref[PAIR:EXT, :] = tail.astype(BF16)
            if group != A:
                tail_ref = left_tail_ref if group == LEFT else b_tail_ref
                tail_ref[:, to] = jnp.where(tail_used, tail, 0.0).astype(BF16)
            values.append(value_ref)
        left, a, b = (ref[...] for ref in values)
        a_ref[:, to] = a
        scores = (nt(a, b) * mask).astype(BF16)
        kept_ref[:, to] = nn(scores, left)
        front_ref[:, to] = raw_ref[0 : PRE + 8, :]
        sums = [jnp.zeros((8, HEAD), F32)] * TAPS
        for first in range(0, PAIR, 64):
            kept = kept_ref[first : first + 64, to]
            for j in range(TAPS):
                start = PRE + first - j
                term = kept * raw_ref[start : start + 64, :]
                sums[j] = sums[j] + jnp.sum(term.reshape(8, 8, HEAD), 0)
        terms_ref[:, to] = jnp.concatenate([jnp.sum(s, 0, keepdims=True) for s in sums], 0)


def terms_kernel(
    scalars, terms_ref, products_ref, a_ref, front_ref, left_tail_ref, b_tail_ref,
    near_one_ref, near_two_ref, far_one_ref, far_two_ref, wrap_ref, taps_ref, fold_ref, rows_ref,
    states_ref, shares_ref, edge_ref, seam_ref, total_ref, stack_ref,
):
    core = scalars[0]
    heads, width = products_ref.shape[0], terms_ref.shape[1]
    none = jnp.zeros((8, HEAD), F32)
    for head in range(heads):
        to = lanes(0, head, width)
        near_ref, at = half_of(near_one_ref, near_two_ref, head)
        far_ref, _ = half_of(far_one_ref, far_two_ref, head)
        near, far = (r[at, HEAD : HEAD + 2 * EDGE, :].astype(F32) for r in (near_ref, far_ref))
        wrap = wrap_ref[head, HEAD:, :].astype(F32)
        near = jnp.where(core == 0, near[0:EDGE], near[EDGE : 2 * EDGE])
        first, last = far[0:EDGE], far[EDGE : 2 * EDGE]
        for turn, (zero, one) in enumerate((((last, near), (near, first)), ((wrap, first), (last, wrap)))):
            before, after = (jnp.where(core == 0, *pair) for pair in zip(zero, one))
            for slot, at in enumerate((slice(0, 4), slice(4, 8))):
                edge_ref[2 * slot + turn, 0:8, to] = jnp.concatenate([before[at], after[at]], 0)
                edge_ref[2 * slot + turn, 8:16, to] = none
    row = lax.broadcasted_iota(jnp.int32, (8, width), 0)
    for slot, group, tail_ref in ((0, LEFT, left_tail_ref), (1, B, b_tail_ref)):
        taps = taps_ref[:, group * width : (group + 1) * width]
        rows = [convolved(edge_ref.at[2 * slot + turn], taps, 4, 8) for turn in range(2)]
        rows = [jnp.where(row < TAPS - 1, total, 0.0) for total in rows]
        seam_ref[slot, 0:16, :] = jnp.concatenate(rows, 0).astype(BF16)
        seam_ref[slot, 16:32, :] = tail_ref[...]
    every = [(head, lanes(0, head, width)) for head in range(heads)]
    seams = [tn(seam_ref[1, :, to], seam_ref[0, :, to]) for _, to in every]
    states = []
    for (head, _), seam in zip(every, seams):
        near_ref, at = half_of(near_one_ref, near_two_ref, head)
        far_ref, _ = half_of(far_one_ref, far_two_ref, head)
        near, far = (r[at, 0:HEAD, :].astype(F32) for r in (near_ref, far_ref))
        wrap = wrap_ref[head, 0:HEAD, :].astype(F32)
        states.append((near + far + (wrap + seam)).astype(BF16))
    fronts = [nn(a_ref[0:16, to], state) for (_, to), state in zip(every, states)]
    row = lax.broadcasted_iota(jnp.int32, (8, HEAD), 0)
    for (head, to), state, front in zip(every, states, fronts):
        states_ref[head] = state
        state = state.astype(F32)
        front = jnp.where(row < TAPS - 1, front[0:8] * (1.0 / HEAD), 0.0)
        sums = []
        for j in range(TAPS):
            product = (state * products_ref[head, j]).reshape(HEAD // 8, 8, HEAD)
            total = jnp.sum(product, 0) + front * front_ref[PRE - j : PRE - j + 8, to]
            sums.append(jnp.sum(total, 0, keepdims=True))
        total_ref[:, to] = terms_ref[:, to] + jnp.concatenate(sums, 0)
    half = width // 2
    spread = rows_ref.shape[0]
    fitting = rows_ref[...]
    for part in range(2):
        for j in range(TAPS):
            at = (part * TAPS + j) * spread
            line = total_ref[j : j + 1, part * half : (part + 1) * half]
            stack_ref[at : at + spread, :] = fitting * line
    folded = nn(stack_ref[...].astype(BF16), fold_ref[...])
    few = half // spread
    place = lax.broadcasted_iota(jnp.int32, (spread, fold_ref.shape[1]), 1)
    gathered = jnp.zeros((spread, fold_ref.shape[1]), F32)
    for part in range(2):
        for j in range(TAPS):
            at = (part * TAPS + j) * spread
            begin = part * (fold_ref.shape[1] // 2) + j * few
            here = (place >= begin) & (place < begin + few)
            gathered = gathered + jnp.where(here, folded[at : at + spread], 0.0)
    shares_ref[...] = gathered.reshape(shares_ref.shape)


def input_kernel(
    scalars, inside_ref, a_ref, states_ref, taps_ref, after_ref, own_ref, send_ref, grad_ref, kept_ref
):
    core = scalars[0]
    width = own_ref.shape[1]
    for head in range(width // HEAD):
        to = lanes(0, head, width)
        kept_ref[:, to] = inside_ref[:, to] + nn(a_ref[:, to], states_ref[head]) * (1.0 / HEAD)
        taps = taps_ref[:, lanes(RAW, head, width)]
        for first in range(0, PAIR, 64):
            grad = taps[0:1] * kept_ref[first : first + 64, to]
            for j in range(1, TAPS):
                grad = grad + taps[j : j + 1] * kept_ref[first + j : first + j + 64, to]
            grad_ref[first : first + 64, to] = grad.astype(BF16)
    own_ref[...] = grad_ref[pl.ds(pl.multiple_of(core * ROWS, ROWS), ROWS), :]
    send_ref[...] = grad_ref[pl.ds(pl.multiple_of((1 - core) * ROWS, ROWS), ROWS), :]


def join_kernel(scalars, own_ref, other_ref, out_ref):
    width = own_ref.shape[1]
    for core, parts in enumerate(((own_ref, other_ref), (other_ref, own_ref))):

        @pl.when(scalars[0] == core)
        def _():
            for half, part in enumerate(parts):
                out_ref[:, half * width : (half + 1) * width] = part[...]


def per_device(qkv_input, conv_weight, out_cotangent):
    x, g = qkv_input[0], out_cotangent[0]
    width = g.shape[1] // 2
    heads = width // HEAD
    chips = lax.axis_size("zh")
    core, chip, low = lax.axis_index("core"), lax.axis_index("zh"), lax.axis_index("zl")
    scalars = jnp.stack([core, chip]).astype(jnp.int32)
    fitting = (jnp.arange(8 * chips) // (4 * chips) == low // 2).astype(F32)[:, None]
    swap = [(0, 1), (1, 0)]
    line = ("zh", "core")

    def hops(by):
        later = [(2 * c, 2 * (c + by)) for c in range(chips - by)]
        return later + [(2 * (c + by) + 1, 2 * c + 1) for c in range(chips - by)]

    keep, send = call(
        pack_kernel, [((rows, 4 * width), BF16) for rows in (ROWS, ROWS + 16)],
        [pltpu.SemaphoreType.DMA((8,))],
        scalars, *(pltpu.with_memory_space_constraint(each, pltpu.HBM) for each in (x, g)), fitting,
        space=pl.BlockSpec(memory_space=pl.ANY), limit=8,
    )
    (taps,) = call(taps_kernel, [((TAPS, 4 * width), F32)], [], scalars, conv_weight)
    received = lax.ppermute(send, "core", swap)
    padded = [pltpu.VMEM((LONG, HEAD), F32)] * 4
    message, second = (((many, HEAD + 4 * EDGE, HEAD), BF16) for many in (6 * heads // 10, heads - 6 * heads // 10))
    buffers = padded + [pltpu.VMEM((PAIR, HEAD), BF16)] * 4
    (one,) = call(states_kernel, [message], buffers, scalars, keep, received, taps)
    near_one = lax.ppermute(one, line, hops(1))
    spread = lax.axis_size("yx")
    few = width // 2 // spread
    part = -(-TAPS * few // HEAD) * HEAD
    tail = ((16, width), BF16)
    products, fold, rows = call(
        products_kernel,
        [
            ((heads, TAPS, HEAD, HEAD), F32), ((width // 2, 2 * part), BF16),
            ((spread, width // 2), F32),
        ],
        padded, scalars, keep, received, taps, one,
    )
    (two,) = call(
        second_states_kernel, [second], buffers, scalars, keep, received, taps, one, fold
    )
    near_two = lax.ppermute(two, line, hops(1))
    (wrap,) = call(wrap_kernel, [((heads, HEAD + EDGE, HEAD), BF16)], [], scalars, one, two)
    wrap = lax.ppermute(wrap, line, hops(3))
    onward = [pair for pair in hops(1) if pair not in ((0, 2), (2 * chips - 1, 2 * chips - 3))]
    far_one, far_two = (
        lax.ppermute(call(
            hand_on_kernel, [((near.shape[0], HEAD + 2 * EDGE, HEAD), BF16)], [], scalars, near, fold
        )[0], line, onward)
        for near in (near_one, near_two)
    )
    (partner,) = call(
        partner_kernel, [((4, 3 * width), BF16)], [], scalars, near_one, near_two
    )
    partner = lax.ppermute(partner, "core", swap)
    inside, a, left_tail, b_tail, terms, front = call(
        inside_kernel,
        [
            ((EXT, width), F32), ((EXT, width), BF16), tail, tail, ((TAPS, width), F32),
            ((PRE + 8, width), F32),
        ],
        padded + [pltpu.VMEM((EXT, HEAD), BF16)] * 4,
        scalars, keep, received, near_one, near_two, partner, taps,
    )
    states, rows = call(
        terms_kernel, [((heads, HEAD, HEAD), BF16), ((spread, 1, 2 * part), F32)],
        [
            pltpu.VMEM((4, 16, width), F32), pltpu.VMEM((2, 32, width), BF16),
            pltpu.VMEM((TAPS, width), F32), pltpu.VMEM((2 * TAPS * spread, width // 2), F32),
        ],
        scalars, terms, products, a, front, left_tail, b_tail,
        near_one, near_two, far_one, far_two, wrap, taps, fold, rows,
    )
    rows = jnp.sum(lax.all_to_all(rows, "yx", 0, 0, tiled=True), (0, 1)).reshape(2, part)
    rows = jnp.broadcast_to(rows[None, None, :, None], (2, 2, 2, chips, part)).reshape(8 * chips, part)
    own, sent = call(
        input_kernel, [((ROWS, width), BF16)] * 2,
        [pltpu.VMEM((PAIR, width), BF16), pltpu.VMEM((EXT, width), F32)],
        scalars, inside, a, states, taps, rows,
    )
    rows = lax.all_to_all(rows, ("core", "zl", "zh"), 0, 0, tiled=True)
    other = lax.ppermute(sent, "core", swap)
    (grad,) = call(join_kernel, [((ROWS, 2 * width), BF16)], [], scalars, own, other)
    share = jnp.sum(rows * fitting, 0)[: TAPS * few].reshape(TAPS, few)
    return grad[None], share * (1.0 / (lax.axis_size("zl") * spread))


def solution(mesh):
    dp, seq = mesh.shape["dp"], mesh.shape["seq"]
    fine = Mesh(mesh.devices.reshape(4, dp // 4, seq // 2, 2), ("zl", "yx", "zh", "core"))
    rows = P(("zl", "yx"), ("zh", "core"), None)
    return jax.shard_map(
        per_device, mesh=fine, in_specs=(rows, P(), rows),
        out_specs=(rows, P(None, ("zl", "yx"))), check_vma=False,
    )
```

```python
import jax
import jax.numpy as jnp
from jax import lax
from jax.experimental import pallas as pl
from jax.experimental.pallas import tpu as pltpu
from jax.sharding import Mesh
from jax.sharding import PartitionSpec as P

HEAD = 128
TAPS = 4
ROWS = 128
PAIR = 2 * ROWS
EXT = PAIR + 16
PRE = 8
LONG = PRE + PAIR + 8
EDGE = 8
F32 = jnp.float32
BF16 = jnp.bfloat16
LEFT, A, B, RAW = range(4)
VMEM = pl.BlockSpec(memory_space=pltpu.VMEM)
SMEM = pl.BlockSpec(memory_space=pltpu.SMEM)


def call(kernel, shapes, scratch, scalars, *arrays, space=VMEM, limit=16):
    return pl.pallas_call(
        kernel,
        out_shape=[jax.ShapeDtypeStruct(s, t) for s, t in shapes],
        in_specs=[SMEM] + [space] * len(arrays),
        out_specs=[VMEM] * len(shapes),
        scratch_shapes=scratch,
        compiler_params=pltpu.CompilerParams(vmem_limit_bytes=limit * 1024 * 1024),
    )(scalars, *arrays)


def nt(a, b):
    return lax.dot_general(a, b, (((1,), (1,)), ((), ())), preferred_element_type=F32)


def tn(a, b):
    return lax.dot_general(a, b, (((0,), (0,)), ((), ())), preferred_element_type=F32)


def nn(a, b):
    return lax.dot_general(a, b, (((1,), (0,)), ((), ())), preferred_element_type=F32)


def lanes(group, head, width):
    return slice(group * width + head * HEAD, group * width + (head + 1) * HEAD)


def fill_edges(core, keep_ref, send_ref):
    width = keep_ref.shape[1] // 4
    edge = pl.ds(pl.multiple_of(core * (ROWS - 16), 16), 16)
    none = jnp.zeros((12, width), F32)
    for slot, (first, last) in enumerate(((LEFT, LEFT), (A, A), (B, RAW), (RAW, RAW))):
        zero = keep_ref[edge, first * width : (first + 1) * width].astype(F32)[0:4]
        one = keep_ref[edge, last * width : (last + 1) * width].astype(F32)[12:16]
        rows = jnp.concatenate([jnp.where(core == 1, one, zero), none], 0)
        send_ref[ROWS : ROWS + 16, slot * width : (slot + 1) * width] = rows.astype(BF16)


def pack_kernel(scalars, x_ref, g_ref, before_ref, keep_ref, send_ref, sems):
    core = scalars[0]
    width = keep_ref.shape[1] // 4
    of_core = (
        ((x_ref, 3), (g_ref, 1), (x_ref, 5), (x_ref, 1)),
        ((x_ref, 0), (x_ref, 4), (g_ref, 0), (x_ref, 2)),
    )

    def fill(mine):
        copies = []

        def copy(source_ref, group, out_ref, slot):
            lanes_in = slice(group * width, (group + 1) * width)
            lanes_out = slice(slot * width, (slot + 1) * width)
            copies.append(
                pltpu.make_async_copy(
                    source_ref.at[:, lanes_in], out_ref.at[0:ROWS, lanes_out], sems.at[len(copies)]
                )
            )

        for slot, (source_ref, group) in enumerate(of_core[1 - mine]):
            copy(source_ref, group, send_ref, slot)
        for slot, (source_ref, group) in enumerate(of_core[mine]):
            copy(source_ref, group, keep_ref, slot)
        for each in copies:
            each.start()
        for each in copies:
            each.wait()

    @pl.when(core == 0)
    def _():
        fill(0)

    @pl.when(core == 1)
    def _():
        fill(1)

    fill_edges(core, keep_ref, send_ref)


def taps_kernel(scalars, w_ref, taps_ref):
    width = taps_ref.shape[1] // 4
    row = lax.broadcasted_iota(jnp.int32, (TAPS, width), 0)
    unit = jnp.where(row == 0, 1.0, 0.0).astype(F32)
    for core, groups in enumerate(((3, None, 5, 1), (0, 4, None, 2))):

        @pl.when(scalars[0] == core)
        def _():
            for slot, group in enumerate(groups):
                part = unit if group is None else w_ref[:, group * width : (group + 1) * width]
                taps_ref[:, slot * width : (slot + 1) * width] = part


def gather_rows(core, keep_ref, received_ref, at, padded_ref):
    own = pl.ds(pl.multiple_of(PRE + core * ROWS, 8), ROWS)
    other = pl.ds(pl.multiple_of(PRE + (1 - core) * ROWS, 8), ROWS)
    padded_ref[own, :] = keep_ref[:, at].astype(F32)
    padded_ref[other, :] = received_ref[0:ROWS, at].astype(F32)


def convolved(padded_ref, taps, start, count):
    total = taps[0:1] * padded_ref[start : start + count, :]
    for j in range(1, TAPS):
        total = total + taps[j : j + 1] * padded_ref[start - j : start - j + count, :]
    return total


def half_of(one_ref, two_ref, head):
    first = one_ref.shape[0]
    return (one_ref, head) if head < first else (two_ref, head - first)


def states_kernel(scalars, keep_ref, received_ref, taps_ref, message_ref, *scratch, begin=0):
    core, chip = scalars[0], scalars[1]
    width = keep_ref.shape[1] // 4
    padded_refs, value_refs = scratch[:4], scratch[4:]
    for ref in padded_refs:
        ref[0:PRE, :] = jnp.zeros((PRE, HEAD), F32)
    row = lax.broadcasted_iota(jnp.int32, (ROWS, HEAD), 0)
    kept_rows = (row >= TAPS - 1) | (chip == 0)
    first_rows = jnp.where(chip == 0, 0.0, 1.0)
    for place in range(message_ref.shape[0]):
        head = begin + place
        firsts, lasts = [], []
        for turn, group in enumerate((LEFT, B)):
            padded_ref = padded_refs[(2 * head + turn) % 4]
            value_ref = value_refs[(2 * head + turn) % 4]
            at = lanes(group, head, width)
            gather_rows(core, keep_ref, received_ref, at, padded_ref)
            taps = taps_ref[:, at]
            for first in (0, ROWS):
                total = convolved(padded_ref, taps, PRE + first, ROWS)
                if group == LEFT and first == 0:
                    total = jnp.where(kept_rows, total, 0.0)
                value_ref[first : first + ROWS, :] = total.astype(BF16)
            front = padded_ref[PRE : PRE + 4, :]
            firsts.append(front * first_rows if group == LEFT else front)
            lasts.append(padded_ref[PRE + PAIR - 4 : PRE + PAIR, :])
        left, right = value_refs[(2 * head) % 4], value_refs[(2 * head + 1) % 4]
        message_ref[place, 0:HEAD, :] = tn(right[...], left[...]).astype(BF16)
        third = jnp.where(
            core == 0,
            received_ref[ROWS - 16 : ROWS, lanes(RAW, head, width)].astype(F32)[12:16],
            received_ref[0:16, lanes(A, head, width)].astype(F32)[0:4],
        )
        others = [
            received_ref[ROWS : ROWS + 16, lanes(slot, head, width)].astype(F32)[0:4] for slot in range(3)
        ]
        message_ref[place, HEAD:, :] = jnp.concatenate([*firsts, *lasts, third, *others], 0).astype(BF16)


def second_states_kernel(
    scalars, keep_ref, received_ref, taps_ref, one_ref, two_ref, *scratch
):
    states_kernel(scalars, keep_ref, received_ref, taps_ref, two_ref, *scratch, begin=one_ref.shape[0])


def wrap_kernel(scalars, one_ref, two_ref, wrap_ref):
    for head in range(wrap_ref.shape[0]):
        message_ref, at = half_of(one_ref, two_ref, head)
        wrap_ref[head, 0:HEAD, :] = message_ref[at, 0:HEAD, :]
        edges = message_ref[at, HEAD : HEAD + 2 * EDGE, :].astype(F32)
        edges = jnp.where(scalars[0] == 0, edges[EDGE:], edges[:EDGE])
        wrap_ref[head, HEAD:, :] = edges.astype(BF16)


def partner_kernel(scalars, near_one_ref, near_two_ref, out_ref):
    width = out_ref.shape[1] // 3
    for head in range(width // HEAD):
        near_ref, at = half_of(near_one_ref, near_two_ref, head)
        rows = near_ref[at, HEAD + 2 * EDGE :, :].astype(F32)
        for slot in range(3):
            out_ref[:, lanes(slot, head, width)] = rows[4 * slot + 4 : 4 * slot + 8].astype(BF16)


def hand_on_kernel(scalars, message_ref, after_ref, out_ref):
    out_ref[...] = message_ref[:, 0 : out_ref.shape[1], :]


def products_kernel(
    scalars, keep_ref, received_ref, taps_ref, after_ref, products_ref, fold_ref, rows_ref, *padded_refs
):
    core = scalars[0]
    width = keep_ref.shape[1] // 4
    for ref in padded_refs:
        ref[0:PRE, :] = jnp.zeros((PRE, HEAD), F32)
    row = lax.broadcasted_iota(jnp.int32, (PAIR, HEAD), 0)
    for head in range(width // HEAD):
        a_ref, raw_ref = (padded_refs[(2 * head + k) % 4] for k in range(2))
        at = lanes(A, head, width)
        gather_rows(core, keep_ref, received_ref, at, a_ref)
        gather_rows(core, keep_ref, received_ref, lanes(RAW, head, width), raw_ref)
        a = convolved(a_ref, taps_ref[:, at], PRE, PAIR)
        a = jnp.where(row >= TAPS - 1, a, 0.0).astype(BF16)
        for j in range(TAPS):
            shifted = raw_ref[PRE - j : PRE - j + PAIR, :].astype(BF16)
            products_ref[head, j] = tn(a, shifted) * (1.0 / HEAD)
    few = width // 2 // rows_ref.shape[0]
    place = lax.broadcasted_iota(jnp.int32, fold_ref.shape, 1)
    column = lax.broadcasted_iota(jnp.int32, fold_ref.shape, 0)
    place = lax.rem(place, fold_ref.shape[1] // 2)
    fits = (lax.rem(column, few) == lax.rem(place, few)) & (place < TAPS * few)
    fold_ref[...] = jnp.where(fits, 1.0, 0.0).astype(BF16)
    device = lax.broadcasted_iota(jnp.int32, rows_ref.shape, 0) * few
    column = lax.broadcasted_iota(jnp.int32, rows_ref.shape, 1)
    rows_ref[...] = jnp.where((column >= device) & (column < device + few), 1.0, 0.0)


def inside_kernel(
    scalars, keep_ref, received_ref, near_one_ref, near_two_ref, other_ref, taps_ref,
    kept_ref, a_ref, left_tail_ref, b_tail_ref, terms_ref, front_ref, *scratch,
):
    core = scalars[0]
    width = keep_ref.shape[1] // 4
    padded_refs, value_refs = scratch[:4], scratch[4:]
    other = other_ref[...].astype(F32)
    row = lax.broadcasted_iota(jnp.int32, (EXT, EXT), 0)
    column = lax.broadcasted_iota(jnp.int32, (EXT, EXT), 1)
    causal = jnp.where(column <= row, 1.0 / HEAD, 0.0)
    reverse = jnp.where(
        (column >= row) & (column < PAIR),
        1.0 / HEAD,
        jnp.where((column >= PAIR) & (column < row), -1.0 / HEAD, 0.0),
    )
    mask = jnp.where(core == 0, causal, reverse)
    none = jnp.zeros((4, HEAD), F32)
    tail_row = lax.broadcasted_iota(jnp.int32, (16, HEAD), 0)
    tail_used = (tail_row < TAPS - 1) & (core == 1)
    turn = 0
    for head in range(width // HEAD):
        to = lanes(0, head, width)
        values = []
        near_ref, half = half_of(near_one_ref, near_two_ref, head)
        near = near_ref[half, HEAD:, :].astype(F32)
        first, last, third = near[0:EDGE], near[EDGE : 2 * EDGE], near[2 * EDGE : 2 * EDGE + 4]
        partner = [other[:, lanes(slot, head, width)] for slot in range(3)]
        befores = zip((last[0:4], third, last[4:8], third), (partner[0], partner[1], partner[1], partner[2]))
        afters = zip((partner[0], partner[1], partner[2], third), (first[0:4], third, first[4:8], third))
        befores, afters = ([jnp.where(core == 0, *pair) for pair in pairs] for pairs in (befores, afters))
        for group in (LEFT, A, B, RAW):
            padded_ref = padded_refs[turn % 4]
            value_ref = value_refs[turn % 4]
            turn += 1
            at = lanes(group, head, width)
            gather_rows(core, keep_ref, received_ref, at, padded_ref)
            padded_ref[0:PRE, :] = jnp.concatenate([none, befores[group]], 0)
            padded_ref[PRE + PAIR : LONG, :] = jnp.concatenate([afters[group], none], 0)
            if group == RAW:
                raw_ref = padded_ref
                continue
            taps = taps_ref[:, at]
            for first in (0, ROWS):
                total = convolved(padded_ref, taps, PRE + first, ROWS)
                value_ref[first : first + ROWS, :] = total.astype(BF16)
            tail = convolved(padded_ref, taps, PRE + PAIR, 8)
            tail = jnp.concatenate([tail, jnp.zeros((8, HEAD), F32)], 0)
            value_ref[PAIR:EXT, :] = tail.astype(BF16)
            if group != A:
                tail_ref = left_tail_ref if group == LEFT else b_tail_ref
                tail_ref[:, to] = jnp.where(tail_used, tail, 0.0).astype(BF16)
            values.append(value_ref)
        left, a, b = (ref[...] for ref in values)
        a_ref[:, to] = a
        scores = (nt(a, b) * mask).astype(BF16)
        kept_ref[:, to] = nn(scores, left)
        front_ref[:, to] = raw_ref[0 : PRE + 8, :]
        sums = [jnp.zeros((8, HEAD), F32)] * TAPS
        for first in range(0, PAIR, 64):
            kept = kept_ref[first : first + 64, to]
            for j in range(TAPS):
                start = PRE + first - j
                term = kept * raw_ref[start : start + 64, :]
                sums[j] = sums[j] + jnp.sum(term.reshape(8, 8, HEAD), 0)
        terms_ref[:, to] = jnp.concatenate([jnp.sum(s, 0, keepdims=True) for s in sums], 0)


def terms_kernel(
    scalars, terms_ref, products_ref, a_ref, front_ref, left_tail_ref, b_tail_ref,
    near_one_ref, near_two_ref, far_one_ref, far_two_ref, wrap_ref, taps_ref, fold_ref, rows_ref,
    states_ref, shares_ref, edge_ref, seam_ref, total_ref, stack_ref,
):
    core = scalars[0]
    heads, width = products_ref.shape[0], terms_ref.shape[1]
    none = jnp.zeros((8, HEAD), F32)
    for head in range(heads):
        to = lanes(0, head, width)
        near_ref, at = half_of(near_one_ref, near_two_ref, head)
        far_ref, _ = half_of(far_one_ref, far_two_ref, head)
        near, far = (r[at, HEAD : HEAD + 2 * EDGE, :].astype(F32) for r in (near_ref, far_ref))
        wrap = wrap_ref[head, HEAD:, :].astype(F32)
        near = jnp.where(core == 0, near[0:EDGE], near[EDGE : 2 * EDGE])
        first, last = far[0:EDGE], far[EDGE : 2 * EDGE]
        for turn, (zero, one) in enumerate((((last, near), (near, first)), ((wrap, first), (last, wrap)))):
            before, after = (jnp.where(core == 0, *pair) for pair in zip(zero, one))
            for slot, at in enumerate((slice(0, 4), slice(4, 8))):
                edge_ref[2 * slot + turn, 0:8, to] = jnp.concatenate([before[at], after[at]], 0)
                edge_ref[2 * slot + turn, 8:16, to] = none
    row = lax.broadcasted_iota(jnp.int32, (8, width), 0)
    for slot, group, tail_ref in ((0, LEFT, left_tail_ref), (1, B, b_tail_ref)):
        taps = taps_ref[:, group * width : (group + 1) * width]
        rows = [convolved(edge_ref.at[2 * slot + turn], taps, 4, 8) for turn in range(2)]
        rows = [jnp.where(row < TAPS - 1, total, 0.0) for total in rows]
        seam_ref[slot, 0:16, :] = jnp.concatenate(rows, 0).astype(BF16)
        seam_ref[slot, 16:32, :] = tail_ref[...]
    every = [(head, lanes(0, head, width)) for head in range(heads)]
    seams = [tn(seam_ref[1, :, to], seam_ref[0, :, to]) for _, to in every]
    states = []
    for (head, _), seam in zip(every, seams):
        near_ref, at = half_of(near_one_ref, near_two_ref, head)
        far_ref, _ = half_of(far_one_ref, far_two_ref, head)
        near, far = (r[at, 0:HEAD, :].astype(F32) for r in (near_ref, far_ref))
        wrap = wrap_ref[head, 0:HEAD, :].astype(F32)
        states.append((near + far + (wrap + seam)).astype(BF16))
    fronts = [nn(a_ref[0:16, to], state) for (_, to), state in zip(every, states)]
    row = lax.broadcasted_iota(jnp.int32, (8, HEAD), 0)
    for (head, to), state, front in zip(every, states, fronts):
        states_ref[head] = state
        state = state.astype(F32)
        front = jnp.where(row < TAPS - 1, front[0:8] * (1.0 / HEAD), 0.0)
        sums = []
        for j in range(TAPS):
            product = (state * products_ref[head, j]).reshape(HEAD // 8, 8, HEAD)
            total = jnp.sum(product, 0) + front * front_ref[PRE - j : PRE - j + 8, to]
            sums.append(jnp.sum(total, 0, keepdims=True))
        total_ref[:, to] = terms_ref[:, to] + jnp.concatenate(sums, 0)
    half = width // 2
    spread = rows_ref.shape[0]
    fitting = rows_ref[...]
    for part in range(2):
        for j in range(TAPS):
            at = (part * TAPS + j) * spread
            line = total_ref[j : j + 1, part * half : (part + 1) * half]
            stack_ref[at : at + spread, :] = fitting * line
    folded = nn(stack_ref[...].astype(BF16), fold_ref[...])
    few = half // spread
    place = lax.broadcasted_iota(jnp.int32, (spread, fold_ref.shape[1]), 1)
    gathered = jnp.zeros((spread, fold_ref.shape[1]), F32)
    for part in range(2):
        for j in range(TAPS):
            at = (part * TAPS + j) * spread
            begin = part * (fold_ref.shape[1] // 2) + j * few
            here = (place >= begin) & (place < begin + few)
            gathered = gathered + jnp.where(here, folded[at : at + spread], 0.0)
    shares_ref[...] = gathered.reshape(shares_ref.shape)


def input_kernel(
    scalars, inside_ref, a_ref, states_ref, taps_ref, after_ref, own_ref, send_ref, grad_ref, kept_ref
):
    core = scalars[0]
    width = own_ref.shape[1]
    for head in range(width // HEAD):
        to = lanes(0, head, width)
        kept_ref[:, to] = inside_ref[:, to] + nn(a_ref[:, to], states_ref[head]) * (1.0 / HEAD)
        taps = taps_ref[:, lanes(RAW, head, width)]
        for first in range(0, PAIR, 64):
            grad = taps[0:1] * kept_ref[first : first + 64, to]
            for j in range(1, TAPS):
                grad = grad + taps[j : j + 1] * kept_ref[first + j : first + j + 64, to]
            grad_ref[first : first + 64, to] = grad.astype(BF16)
    own_ref[...] = grad_ref[pl.ds(pl.multiple_of(core * ROWS, ROWS), ROWS), :]
    send_ref[...] = grad_ref[pl.ds(pl.multiple_of((1 - core) * ROWS, ROWS), ROWS), :]


def join_kernel(scalars, own_ref, other_ref, out_ref):
    width = own_ref.shape[1]
    for core, parts in enumerate(((own_ref, other_ref), (other_ref, own_ref))):

        @pl.when(scalars[0] == core)
        def _():
            for half, part in enumerate(parts):
                out_ref[:, half * width : (half + 1) * width] = part[...]


def per_device(qkv_input, conv_weight, out_cotangent):
    x, g = qkv_input[0], out_cotangent[0]
    width = g.shape[1] // 2
    heads = width // HEAD
    chips = lax.axis_size("zh")
    core, chip, low = lax.axis_index("core"), lax.axis_index("zh"), lax.axis_index("zl")
    scalars = jnp.stack([core, chip]).astype(jnp.int32)
    fitting = (jnp.arange(8 * chips) // (4 * chips) == low // 2).astype(F32)[:, None]
    swap = [(0, 1), (1, 0)]
    line = ("zh", "core")

    def hops(by):
        later = [(2 * c, 2 * (c + by)) for c in range(chips - by)]
        return later + [(2 * (c + by) + 1, 2 * c + 1) for c in range(chips - by)]

    keep, send = call(
        pack_kernel, [((rows, 4 * width), BF16) for rows in (ROWS, ROWS + 16)],
        [pltpu.SemaphoreType.DMA((8,))],
        scalars, *(pltpu.with_memory_space_constraint(each, pltpu.HBM) for each in (x, g)), fitting,
        space=pl.BlockSpec(memory_space=pl.ANY), limit=8,
    )
    (taps,) = call(taps_kernel, [((TAPS, 4 * width), F32)], [], scalars, conv_weight)
    received = lax.ppermute(send, "core", swap)
    padded = [pltpu.VMEM((LONG, HEAD), F32)] * 4
    message, second = (((many, HEAD + 4 * EDGE, HEAD), BF16) for many in (6 * heads // 10, heads - 6 * heads // 10))
    buffers = padded + [pltpu.VMEM((PAIR, HEAD), BF16)] * 4
    (one,) = call(states_kernel, [message], buffers, scalars, keep, received, taps)
    near_one = lax.ppermute(one, line, hops(1))
    spread = lax.axis_size("yx")
    few = width // 2 // spread
    part = -(-TAPS * few // HEAD) * HEAD
    tail = ((16, width), BF16)
    products, fold, rows = call(
        products_kernel,
        [
            ((heads, TAPS, HEAD, HEAD), F32), ((width // 2, 2 * part), BF16),
            ((spread, width // 2), F32),
        ],
        padded, scalars, keep, received, taps, one,
    )
    (two,) = call(
        second_states_kernel, [second], buffers, scalars, keep, received, taps, one
    )
    near_two = lax.ppermute(two, line, hops(1))
    (wrap,) = call(wrap_kernel, [((heads, HEAD + EDGE, HEAD), BF16)], [], scalars, one, two)
    wrap = lax.ppermute(wrap, line, hops(3))
    onward = [pair for pair in hops(1) if pair not in ((0, 2), (2 * chips - 1, 2 * chips - 3))]
    far_one, far_two = (
        lax.ppermute(call(
            hand_on_kernel, [((near.shape[0], HEAD + 2 * EDGE, HEAD), BF16)], [], scalars, near, fold
        )[0], line, onward)
        for near in (near_one, near_two)
    )
    (partner,) = call(
        partner_kernel, [((4, 3 * width), BF16)], [], scalars, near_one, near_two
    )
    partner = lax.ppermute(partner, "core", swap)
    inside, a, left_tail, b_tail, terms, front = call(
        inside_kernel,
        [
            ((EXT, width), F32), ((EXT, width), BF16), tail, tail, ((TAPS, width), F32),
            ((PRE + 8, width), F32),
        ],
        padded + [pltpu.VMEM((EXT, HEAD), BF16)] * 4,
        scalars, keep, received, near_one, near_two, partner, taps,
    )
    states, rows = call(
        terms_kernel, [((heads, HEAD, HEAD), BF16), ((spread, 1, 2 * part), F32)],
        [
            pltpu.VMEM((4, 16, width), F32), pltpu.VMEM((2, 32, width), BF16),
            pltpu.VMEM((TAPS, width), F32), pltpu.VMEM((2 * TAPS * spread, width // 2), F32),
        ],
        scalars, terms, products, a, front, left_tail, b_tail,
        near_one, near_two, far_one, far_two, wrap, taps, fold, rows,
    )
    rows = jnp.sum(lax.all_to_all(rows, "yx", 0, 0, tiled=True), (0, 1)).reshape(2, part)
    rows = jnp.broadcast_to(rows[None, None, :, None], (2, 2, 2, chips, part)).reshape(8 * chips, part)
    own, sent = call(
        input_kernel, [((ROWS, width), BF16)] * 2,
        [pltpu.VMEM((PAIR, width), BF16), pltpu.VMEM((EXT, width), F32)],
        scalars, inside, a, states, taps, rows,
    )
    rows = lax.all_to_all(rows, ("core", "zl", "zh"), 0, 0, tiled=True)
    other = lax.ppermute(sent, "core", swap)
    (grad,) = call(join_kernel, [((ROWS, 2 * width), BF16)], [], scalars, own, other)
    share = jnp.sum(rows * fitting, 0)[: TAPS * few].reshape(TAPS, few)
    return grad[None], share * (1.0 / (lax.axis_size("zl") * spread))


def solution(mesh):
    dp, seq = mesh.shape["dp"], mesh.shape["seq"]
    fine = Mesh(mesh.devices.reshape(4, dp // 4, seq // 2, 2), ("zl", "yx", "zh", "core"))
    rows = P(("zl", "yx"), ("zh", "core"), None)
    return jax.shard_map(
        per_device, mesh=fine, in_specs=(rows, P(), rows),
        out_specs=(rows, P(None, ("zl", "yx"))), check_vma=False,
    )
```
